512 devices in a mesh: fsdp: 16 (over y_hi, z), roll: 32 (over y_lo, x, core).
Axes of the slice: x: 4, y: 8 (y_hi: 2, y_lo: 4; y = y_hi * 4 + y_lo), z: 8, core: 2. Of those that a mesh axis runs over, the one named last changes fastest.
Arguments:
- hidden: bfloat16 [4, 256, 4096], P(None, 'fsdp', 'roll'), may hold values from -6 to 6
- inner_weight: bfloat16 [4096, 8192], P('fsdp', 'roll'), may hold values from -0.09375 to 0.09375
- gate_weight: bfloat16 [4096, 8192], P('fsdp', 'roll'), may hold values from -0.09375 to 0.09375
- group_weight: bfloat16 [4096, 2048], P('fsdp', 'roll'), may hold values from -0.09375 to 0.09375
- step_weight: bfloat16 [4096, 64], P('fsdp', 'roll'), may hold values from -0.09375 to 0.09375
- output_weight: bfloat16 [8192, 4096], P('roll', 'fsdp'), may hold values from -0.125 to 0.125
- filter_inner: float32 [4, 8192], P(None, 'roll'), may hold values from -3 to 3
- filter_inner_bias: float32 [8192], P('roll'), may hold values from -3 to 3
- filter_group: float32 [4, 2048], P(None, 'roll'), may hold values from -3 to 3
- filter_group_bias: float32 [2048], P('roll'), may hold values from -3 to 3
- step_bias: float32 [64], P('roll'), may hold values from -3 to 0.5
- decay_rate: float32 [64], P('roll'), may hold values from 0.02 to 2
- skip_gain: float32 [64], P('roll'), may hold values from 0.5 to 2
- norm_gain: float32 [8192], P('roll'), may hold values from 0.1 to 1.9
- recurrent_state: bfloat16 [256, 64, 128, 256], P('fsdp', 'roll'), may hold values from -6 to 6
- filter_inner_state: bfloat16 [256, 3, 8192], P('fsdp', None, 'roll'), may hold values from -6 to 6
- filter_group_state: bfloat16 [256, 3, 2048], P('fsdp', None, 'roll'), may hold values from -6 to 6
- live_counts: int32 [16], P('fsdp'), may hold values from 8 to 16, as said below
- target_device: int32 [256], P('fsdp'), may hold values from 0 to 15, as said below
- target_slot: int32 [256], P('fsdp'), may hold values from 0 to 15, as said below
Outputs:
- mixer_output: bfloat16 [4, 256, 4096], P(None, 'fsdp', 'roll')
- new_state: bfloat16 [256, 64, 128, 256], P('fsdp', 'roll')
- new_inner_window: bfloat16 [256, 3, 8192], P('fsdp', None, 'roll')
- new_group_window: bfloat16 [256, 3, 2048], P('fsdp', None, 'roll')
The draws below stay inside these ranges and needn't reach their ends.
Inputs may be any that keep to these rules, and one draw needn't show every extreme that they name: Each device's live requests are its first live_counts slots; some device has all 16 slots live and another device has exactly the least. `target_device`: no two live source slots share a destination slot; at most 2 live requests of one device go to one device, and some device sends exactly 2 to some device; entries of slots that are not live are of no meaning. `target_slot`: see target_device.
All inputs are finite; a program needn't handle non-finite values.
Results may differ from the reference program's by a relative error of at most 0.034.
Values may be sent and summed in bfloat16 or wider, within the bound.
A program may use at most 64 MiB of HBM per device.

```python
import math
import jax
import jax.numpy as jnp
from jax import lax

D = 4096
P_SIZE = 128
N = 256
KCONV = 4
HPG = 16
STEPS = 4
SLOTS = 16
REQ = 256
HEADS = 64
GROUPS = 4
CAP = 2


def shuffled_rows(key, count, length):
    return jax.vmap(lambda single: jax.random.permutation(single, length))(jax.random.split(key, count)).astype(jnp.int32)


def routing_plan(key):
    device_count = REQ // SLOTS
    least = max(1, SLOTS // 2)
    key_counts, key_full, key_devices, key_source, key_target, key_least = jax.random.split(key, 6)
    devices = jnp.arange(device_count, dtype=jnp.int32)
    counts_drawn = jax.random.randint(key_counts, (device_count,), least, SLOTS + 1, dtype=jnp.int32)
    fullest = jax.random.randint(key_full, (), 0, device_count, dtype=jnp.int32)
    emptiest = (fullest + 1 + jax.random.randint(key_least, (), 0, device_count - 1, dtype=jnp.int32)) % device_count
    live_counts = jnp.where(devices == fullest, SLOTS, jnp.where(devices == emptiest, least, counts_drawn)).astype(jnp.int32)
    shuffle = jax.random.permutation(key_devices, device_count).astype(jnp.int32)
    source_orders = shuffled_rows(key_source, device_count, SLOTS)
    target_orders = shuffled_rows(key_target, device_count, SLOTS)
    offsets = source_orders // CAP
    target_device = shuffle[(devices[:, None] + offsets) % device_count]
    target_slot = target_orders[target_device, source_orders]
    return (live_counts, target_device.reshape(-1).astype(jnp.int32), target_slot.reshape(-1).astype(jnp.int32))


def draw_live_counts(key, part):
    plan = routing_plan(key)
    return plan[0]


def draw_target_device(key, part):
    plan = routing_plan(key)
    return plan[1]


def draw_target_slot(key, part):
    plan = routing_plan(key)
    return plan[2]


def spiked(array, rng, source, target, parts, factor):
    owner, partner = [(jnp.arange(array.shape[position]) // (array.shape[position] // parts)).reshape([-1 if axis == position else 1 for axis in range(array.ndim)]) for position in (source, target)]
    chosen = jax.random.permutation(rng, parts)[partner]
    strong = (owner == chosen) | (owner == (partner + parts // 2) % parts)
    return jnp.where(strong, factor * array, array)


def block_levels(stream_key, extent, cuts, low, largest):
    def one(axis_at, blocks):
        heights = jax.random.uniform(jax.random.fold_in(jax.random.fold_in(stream_key, 6), axis_at), (blocks,), jnp.float32, low / len(cuts), largest / len(cuts))
        return jnp.repeat(jnp.exp(heights), extent[axis_at] // blocks).reshape((-1,) + (1,) * (len(extent) - axis_at - 1))

    factor_of = one(*cuts[0])
    for cut in cuts[1:]:
        factor_of = factor_of * one(*cut)
    return factor_of


def centred(own_key, dims, spread, most, cuts=(), kind=jnp.bfloat16):
    level = block_levels(own_key, dims, cuts, -0.22, 0.18) if cuts else 1.0
    drawn = jax.random.normal(own_key, dims, jnp.float32) * spread * level
    return jnp.minimum(jnp.maximum(drawn, -most), most).astype(kind)


def noise_with(own_key, dims, width, most, cuts, heavy, held_as=jnp.bfloat16):
    drawn = width * jax.random.normal(own_key, dims, jnp.float32)
    if cuts:
        drawn = drawn * block_levels(own_key, dims, cuts, -0.22, 0.18)
    return jnp.clip(spiked(drawn, jax.random.fold_in(own_key, 3), *heavy), -most, most).astype(held_as)


def setup_inputs(seed: int = 0) -> dict:
    seeds = jax.random.split(jax.random.key(seed), 21)
    return {
        "hidden": centred(seeds[0], (STEPS, REQ, D), 1.0, 6.0, ((1, 16), (2, 32))),
        "inner_weight": centred(seeds[1], (D, HEADS * P_SIZE), D ** -0.5, 0.09375, ((0, 16), (1, 32))),
        "gate_weight": centred(seeds[2], (D, HEADS * P_SIZE), D ** -0.5, 0.09375, ((0, 16), (1, 32))),
        "group_weight": centred(seeds[3], (D, 2 * GROUPS * N), D ** -0.5, 0.09375, ((0, 16), (1, 32))),
        "step_weight": centred(seeds[4], (D, HEADS), D ** -0.5, 0.09375, ((0, 16), (1, 32))),
        "output_weight": noise_with(seeds[5], (HEADS * P_SIZE, D), (HEADS * P_SIZE) ** -0.5, 0.125, ((0, 32), (1, 16)), (0, 1, 32, 2.75)),
        "filter_inner": centred(seeds[6], (KCONV, HEADS * P_SIZE), 0.5, 3.0, ((1, 32),), jnp.float32),
        "filter_inner_bias": centred(seeds[7], (HEADS * P_SIZE,), 0.5, 3.0, ((0, 32),), jnp.float32),
        "filter_group": centred(seeds[8], (KCONV, 2 * GROUPS * N), 0.5, 3.0, ((1, 32),), jnp.float32),
        "filter_group_bias": centred(seeds[9], (2 * GROUPS * N,), 0.5, 3.0, ((0, 32),), jnp.float32),
        "step_bias": jnp.clip(-3.0 + 3.5 * jax.random.uniform(seeds[10], (HEADS,), jnp.float32) ** block_levels(seeds[10], (HEADS,), ((0, 32),), -0.2, 0.2), -3.0, 0.5),
        "decay_rate": jnp.clip(jnp.exp(math.log(2.0) - 4.6051702 * jax.random.uniform(seeds[11], (HEADS,), jnp.float32) ** block_levels(seeds[11], (HEADS,), ((0, 32),), -0.2, 0.2)), 0.02, 2.0),
        "skip_gain": jnp.clip(0.5 + 1.5 * jax.random.uniform(seeds[12], (HEADS,), jnp.float32) ** block_levels(seeds[12], (HEADS,), ((0, 32),), -0.2, 0.2), 0.5, 2.0),
        "norm_gain": jnp.clip(1.0 + 0.18 * jax.random.normal(seeds[13], (HEADS * P_SIZE,), jnp.float32), 0.1, 1.9),
        "recurrent_state": centred(seeds[14], (REQ, HEADS, P_SIZE, N), 1.0, 6.0, ((0, 16), (1, 32))),
        "filter_inner_state": centred(seeds[15], (REQ, KCONV - 1, HEADS * P_SIZE), 1.0, 6.0, ((0, 16), (2, 32))),
        "filter_group_state": centred(seeds[16], (REQ, KCONV - 1, 2 * GROUPS * N), 1.0, 6.0, ((0, 16), (2, 32))),
        "live_counts": draw_live_counts(jax.random.fold_in(seeds[20], 71), 0),
        "target_device": draw_target_device(jax.random.fold_in(seeds[20], 71), 0),
        "target_slot": draw_target_slot(jax.random.fold_in(seeds[20], 71), 0),
    }


eps = 1e-05

def causal_filter(prior, fresh, taps, offset_bias):
    sequence = jnp.concatenate([jnp.transpose(prior, (1, 0, 2)).astype(jnp.float32), fresh.astype(jnp.float32)], axis=0)
    step_count = fresh.shape[0]
    total = jnp.zeros(fresh.shape, jnp.float32)
    for offset in range(taps.shape[0]):
        total = total + taps[offset] * sequence[offset:offset + step_count]
    filtered = jax.nn.silu(total + offset_bias)
    window = jnp.transpose(sequence[step_count:], (1, 0, 2)).astype(jnp.bfloat16)
    return (filtered, window)

def move_rows(values, source_of):
    padded = jnp.concatenate([values, jnp.zeros((1,) + values.shape[1:], values.dtype)], axis=0)
    return padded[source_of]

def reference(hidden, inner_weight, gate_weight, group_weight, step_weight, output_weight, filter_inner, filter_inner_bias, filter_group, filter_group_bias, step_bias, decay_rate, skip_gain, norm_gain, recurrent_state, filter_inner_state, filter_group_state, live_counts, target_device, target_slot):
    slot_ids = jnp.arange(REQ, dtype=jnp.int32)
    owner = (slot_ids // SLOTS).astype(jnp.int32)
    is_live = slot_ids % SLOTS < live_counts[owner]
    target = jnp.where(is_live, target_device * SLOTS + target_slot, REQ).astype(jnp.int32)
    source_of = jnp.full((REQ + 1,), REQ, jnp.int32).at[target].set(slot_ids)[:REQ]
    token_rows = hidden.reshape(STEPS * REQ, D)

    def project(weight):
        product = jnp.dot(token_rows, weight, preferred_element_type=jnp.float32)
        return product.astype(jnp.bfloat16).reshape(STEPS, REQ, weight.shape[1])
    inner_raw = project(inner_weight)
    gate_raw = project(gate_weight)
    group_raw = project(group_weight)
    step_raw = project(step_weight)
    inner_conv, inner_window = causal_filter(move_rows(filter_inner_state, source_of), inner_raw, filter_inner, filter_inner_bias)
    group_conv, group_window = causal_filter(move_rows(filter_group_state, source_of), group_raw, filter_group, filter_group_bias)
    group_sent = lax.optimization_barrier(group_conv.astype(jnp.bfloat16))
    group_conv = group_sent.astype(jnp.float32)
    step_sizes = jax.nn.softplus(step_raw.astype(jnp.float32) + step_bias)
    decays = jnp.exp(-step_sizes * decay_rate)
    basis_cols = GROUPS * N
    input_basis = group_conv[..., :basis_cols].reshape(STEPS, REQ, GROUPS, N)
    output_basis = group_conv[..., basis_cols:].reshape(STEPS, REQ, GROUPS, N)
    inner_heads = inner_conv.reshape(STEPS, REQ, HEADS, P_SIZE)

    def one_head(head_index):
        group_index = head_index // HPG
        start_state = lax.dynamic_index_in_dim(recurrent_state, head_index, 1, keepdims=False)
        carried = move_rows(start_state, source_of).astype(jnp.float32)
        inner_values = lax.dynamic_index_in_dim(inner_heads, head_index, 2, keepdims=False)
        in_basis = lax.dynamic_index_in_dim(input_basis, group_index, 2, keepdims=False)
        out_basis = lax.dynamic_index_in_dim(output_basis, group_index, 2, keepdims=False)
        head_steps = lax.dynamic_index_in_dim(step_sizes, head_index, 2, keepdims=False)
        head_decays = lax.dynamic_index_in_dim(decays, head_index, 2, keepdims=False)
        skip_term = lax.dynamic_index_in_dim(skip_gain, head_index, 0, keepdims=False)
        outputs = []
        for step in range(STEPS):
            carried = carried * head_decays[step][:, None, None] + (head_steps[step][:, None] * inner_values[step])[:, :, None] * in_basis[step][:, None, :]
            readout = jnp.einsum('rpn,rn->rp', carried, out_basis[step], precision=lax.Precision.HIGHEST)
            outputs.append(readout + skip_term * inner_values[step])
        return (jnp.stack(outputs), carried.astype(jnp.bfloat16))
    heads_out, heads_state = lax.map(one_head, jnp.arange(HEADS, dtype=jnp.int32))
    scanned = jnp.transpose(heads_out, (1, 2, 0, 3)).reshape(STEPS, REQ, HEADS * P_SIZE)
    new_state = jnp.transpose(heads_state, (1, 0, 2, 3))
    gated = scanned * jax.nn.silu(gate_raw.astype(jnp.float32))
    grouped = gated.reshape(STEPS, REQ, GROUPS, HPG * P_SIZE)
    scale = lax.rsqrt(lax.optimization_barrier(jnp.mean(grouped * grouped, axis=-1, keepdims=True)) + eps)
    normed = ((grouped * scale).reshape(STEPS, REQ, HEADS * P_SIZE) * norm_gain).astype(jnp.bfloat16)
    mixer_output = jnp.dot(normed.reshape(STEPS * REQ, HEADS * P_SIZE), output_weight, preferred_element_type=jnp.float32)
    mixer_output = mixer_output.astype(jnp.bfloat16).reshape(STEPS, REQ, D)
    return (mixer_output, new_state, inner_window, group_window)
```

```python
import jax
import jax.numpy as jnp
from jax import lax
from jax.experimental import pallas as pl
from jax.experimental.pallas import tpu as pltpu
from jax.sharding import PartitionSpec as P

MESH = pl.DeviceIdType.MESH
F = 16
R = 32
Z = 8
HPG = 16
NSTEP = 4
SLOTS = 16
EPS = 1e-05
F32 = jnp.float32
BF16 = jnp.bfloat16


def peer_of(f, o):
    return ((f // Z + o // Z) % 2) * Z + (f % Z + o % Z) % Z


def source_of(f, o):
    return ((f // Z + o // Z) % 2) * Z + (f % Z + Z - o % Z) % Z


def silu(v):
    return v / (1.0 + jnp.exp(-v))


def dot(a, b, dims):
    return lax.dot_general(a, b, (dims, ((), ())), preferred_element_type=F32)


def kernel(
    idx, hid, wi, wg, wgs, wo, par, winp, state,
    out, new_state, win_i, win_g,
    hid_all, p_send, p_recv, w_recv, w32, st_v, st_send, st_recv, gc_send, gc_recv,
    ga_all, po_send, po_recv, fin_send, fin_recv, acc, ck, bk, uk, yk, ssum, jq,
    h1_s, h1_r, h2_s, h2_r, w_s, w_r, st_s, st_r, p_s, p_r, gc_s, gc_r, ga_s, ga_r, po_s, po_r, fin_s, fin_r, loc,
):
    f = lax.axis_index("fsdp")
    r = lax.axis_index("roll")
    half = r % 2
    home = r // 2

    def remote(src, dst, s, d, device):
        return pltpu.make_async_remote_copy(
            src_ref=src, dst_ref=dst, send_sem=s, recv_sem=d, device_id=device, device_id_type=MESH
        )

    load_state = pltpu.make_async_copy(state, st_v, loc.at[0])
    load_state.start()

    barrier = pltpu.get_barrier_semaphore()

    @pl.loop(1, F)
    def _(o):
        pl.semaphore_signal(barrier, inc=1, device_id=(peer_of(f, o), r), device_id_type=MESH)

    @pl.loop(1, R)
    def _(o):
        pl.semaphore_signal(barrier, inc=1, device_id=(f, (r + o) % R), device_id_type=MESH)

    def is_self(k):
        return (home == f) & (half == k)

    @pl.when(home != f)
    def _():
        for k in range(2):
            pl.semaphore_signal(barrier, inc=1, device_id=(home, 2 * f + k), device_id_type=MESH)

    pl.semaphore_wait(barrier, F - 1 + R - 1 + jnp.where(home != f, 2, 0))

    for k in range(2):

        @pl.when(jnp.logical_not(is_self(k)))
        def _():
            remote(
                hid.at[pl.ds(32 * k, 32)], hid_all.at[2 * f + k, half], h1_s.at[k], h1_r.at[half],
                (home, 2 * f + k),
            ).start()

        @pl.when(is_self(k))
        def _():
            hid_all[r, k] = hid[pl.ds(32 * k, 32), :]

    for k in range(2):

        @pl.when(jnp.logical_not(is_self(k)))
        def _():
            remote(hid.at[pl.ds(0, 32)], hid_all.at[r, k], h1_s.at[k], h1_r.at[k], (f, r)).wait_recv()

    @pl.loop(1, R)
    def _(o):
        to = (r + o) % R
        remote(hid_all.at[r], hid_all.at[r], h2_s.at[to], h2_r.at[r], (f, to)).start()

    @pl.loop(1, F)
    def _(o):
        d = peer_of(f, o)
        remote(winp.at[d], w_recv.at[f], w_s.at[d], w_r.at[f], (d, r)).start()

    w_recv[f] = winp[f]
    load_state.wait()

    @pl.loop(1, F)
    def _(o):
        d = peer_of(f, o)
        for c in range(2):
            st_send[2 * d + c] = st_v[idx[2 * d + c]]
        remote(
            st_send.at[pl.ds(2 * d, 2)], st_recv.at[pl.ds(2 * f, 2)], st_s.at[d], st_r.at[f], (d, r)
        ).start()

    for c in range(2):
        st_recv[2 * f + c] = st_v[idx[2 * f + c]]

    def project(d):
        for h in range(2):
            chunk = 2 * d + h

            @pl.when(chunk != r)
            def _():
                remote(
                    hid_all.at[chunk], hid_all.at[chunk], h2_s.at[chunk], h2_r.at[chunk], (f, r)
                ).wait_recv()

        rows = jnp.concatenate(
            [
                jnp.concatenate([hid_all[2 * d + h, 0], hid_all[2 * d + h, 1]], axis=1)
                for h in range(2)
            ],
            axis=0,
        )
        nn = ((1,), (0,))
        return (
            dot(rows, wi[...], nn).astype(BF16),
            dot(rows, wg[...], nn).astype(BF16),
            dot(rows, wgs[...], nn).astype(BF16),
        )

    @pl.loop(1, F)
    def _(o):
        d = peer_of(f, o)
        a, b, c = project(d)
        p_send[d, :, 0:256] = a
        p_send[d, :, 256:512] = b
        p_send[d, :, 512:640] = c
        remote(p_send.at[d], p_recv.at[f], p_s.at[d], p_r.at[f], (d, r)).start()

    a, b, c = project(f)
    acc[:, 0:256] = a.astype(F32)
    acc[:, 256:512] = b.astype(F32)
    acc[:, 512:640] = c.astype(F32)

    @pl.loop(1, F)
    def _(o):
        s = source_of(f, o)
        remote(winp.at[s], w_recv.at[s], w_s.at[s], w_r.at[s], (f, r)).wait_recv()

    w32[...] = w_recv[...].astype(F32)
    lane = lax.broadcasted_iota(jnp.int32, (F, 128), 1)
    row = lax.broadcasted_iota(jnp.int32, (F, 128), 0)
    placers = []
    code = jnp.zeros((F, 128), F32)
    for c in range(2):
        slot = w32[:, 8 * c + 7, :][:, 64:65].astype(jnp.int32)
        hit = slot == lane
        placers.append(hit.astype(F32).astype(BF16))
        code = code + jnp.where(hit, (2 * row + c + 1).astype(F32), 0.0)

    @pl.loop(0, SLOTS)
    def _(q):
        jq[q] = jnp.sum(jnp.where(lane == q, code, 0.0)).astype(jnp.int32) - 1

    moved = []
    for block in range(8):
        total = jnp.zeros((128, 128), F32)
        for c in range(2):
            total = total + dot(placers[c], w32[:, 8 * c + block, :].astype(BF16), ((0,), (0,)))
        moved.append(total[0:SLOTS])
    prior_i = [jnp.concatenate([moved[2 * k], moved[2 * k + 1]], axis=1) for k in range(3)]
    prior_g = [moved[6], pltpu.roll(moved[6], 64, 1), moved[7]]

    @pl.loop(1, F)
    def _(o):
        s = source_of(f, o)
        remote(p_send.at[s], p_recv.at[s], p_s.at[s], p_r.at[s], (f, r)).wait_recv()
        acc[...] += p_recv[s].astype(F32)

    raw = acc[...].astype(BF16)
    win_i[...] = raw[SLOTS:, 0:256]
    win_g[...] = raw[SLOTS:, 512:640]
    raw = raw.astype(F32)

    def conv(prior, fresh, taps, bias):
        steps = prior + [fresh[SLOTS * t : SLOTS * (t + 1)] for t in range(NSTEP)]
        got = []
        for t in range(NSTEP):
            total = bias
            for k in range(4):
                total = total + taps[k] * steps[t + k]
            got.append(silu(total))
        return got

    group = jnp.concatenate(
        conv(prior_g, raw[:, 512:640], [par[9 + k : 10 + k, 0:128] for k in range(4)], par[13:14, 0:128]),
        axis=0,
    )
    gc_send[...] = jnp.where(half == 1, pltpu.roll(group, 64, 1), group).astype(BF16)
    piece = (r // 16) * 4 + r % 4
    first_user = 8 * ((r % 16) // 4)

    @pl.loop(0, 8)
    def _(m):
        to = first_user + m

        @pl.when(to != r)
        def _():
            remote(gc_send, gc_recv.at[piece], gc_s.at[m], gc_r.at[piece], (f, to)).start()

        @pl.when(to == r)
        def _():
            gc_recv[piece] = gc_send[...]

    xs = conv(prior_i, raw[:, 0:256], [par[k : k + 1] for k in range(4)], par[4:5])
    step_raw = jnp.concatenate(
        [
            jnp.broadcast_to(raw[:, 576:577], (NSTEP * SLOTS, 128)),
            jnp.broadcast_to(raw[:, 577:578], (NSTEP * SLOTS, 128)),
        ],
        axis=1,
    )
    v = step_raw + par[7:8]
    dt = jnp.maximum(v, 0.0) + jnp.log1p(jnp.exp(-jnp.abs(v)))
    dec = jnp.exp(-dt * par[8:9])
    dts = [dt[SLOTS * t : SLOTS * (t + 1)] for t in range(NSTEP)]
    decs = [dec[SLOTS * t : SLOTS * (t + 1)] for t in range(NSTEP)]

    @pl.loop(0, 8)
    def _(i):
        s = (i // 4) * 16 + 4 * (r // 8) + i % 4

        @pl.when(s != r)
        def _():
            remote(gc_send, gc_recv.at[i], gc_s.at[i], gc_r.at[i], (f, r)).wait_recv()

    def basis(i):
        return jnp.concatenate(
            [
                gc_recv[i].astype(F32) + gc_recv[i + 1].astype(F32),
                gc_recv[i + 2].astype(F32) + gc_recv[i + 3].astype(F32),
            ],
            axis=1,
        )

    b_all, c_all = basis(0), basis(4)
    bs = [b_all[SLOTS * t : SLOTS * (t + 1)] for t in range(NSTEP)]
    cs = [c_all[SLOTS * t : SLOTS * (t + 1)] for t in range(NSTEP)]
    us = [dts[t] * xs[t] for t in range(NSTEP)]
    ck[...] = jnp.zeros(ck.shape, F32)
    bk[...] = jnp.zeros(bk.shape, F32)
    uk[...] = jnp.zeros(uk.shape, F32)
    for t in range(NSTEP):
        ck[:, t, :] = cs[t]
        bk[:, t, :] = bs[t]
    tail = None
    for t in reversed(range(NSTEP)):
        uk[:, t, :] = us[t] if tail is None else us[t] * tail
        tail = decs[t] if tail is None else decs[t] * tail
    uk[:, 4, :] = tail

    @pl.loop(1, F)
    def _(o):
        s = source_of(f, o)
        rows = pl.ds(2 * s, 2)
        remote(st_send.at[rows], st_recv.at[rows], st_s.at[s], st_r.at[s], (f, r)).wait_recv()

    @pl.loop(0, SLOTS)
    def _(q):
        j = jq[q]
        start = st_recv[jnp.clip(j, 0, 2 * F - 1)]
        y = dot(ck[q].astype(BF16), start, ((1,), (1,)))
        yk[q] = jnp.where(j >= 0, y, 0.0)

    gates = silu(raw[:, 256:512])
    gated = []
    for t in range(NSTEP):
        total = None
        grown = None
        for s in reversed(range(t + 1)):
            pair = jnp.sum(bs[s] * cs[t], axis=1, keepdims=True)
            term = us[s] * pair
            if grown is not None:
                term = term * grown
            total = term if total is None else total + term
            grown = decs[s] if grown is None else grown * decs[s]
        total = total + grown * yk[:, t, :] + par[6:7] * xs[t]
        gated.append(total * gates[SLOTS * t : SLOTS * (t + 1)])
    ga_all[f] = jnp.concatenate(gated, axis=0).astype(BF16)

    @pl.loop(1, F)
    def _(o):
        d = peer_of(f, o)
        remote(ga_all.at[f], ga_all.at[f], ga_s.at[d], ga_r.at[f], (d, r)).start()

    @pl.loop(0, SLOTS)
    def _(q):
        j = jq[q]
        start = st_recv[jnp.clip(j, 0, 2 * F - 1)].astype(F32)
        start = jnp.where(j >= 0, start, 0.0)
        u = uk[q]
        rate = u[4:5]
        keep = lax.broadcasted_iota(jnp.int32, (8, 256), 0) < 4
        u = jnp.where(keep, u, 0.0)
        high = u.astype(BF16)
        low = (u - high.astype(F32)).astype(BF16)
        b = bk[q].astype(BF16)
        added = dot(
            jnp.concatenate([high, low], axis=0), jnp.concatenate([b, b], axis=0), ((0,), (0,))
        )
        for h in range(2):
            rows = slice(128 * h, 128 * h + 128)
            factor = jnp.concatenate([rate[:, rows], rate[:, rows]], axis=1)
            new_state[q, rows, :] = (start[rows] * factor + added[rows]).astype(BF16)

    def project_out(d):
        g = ga_all[d].astype(F32)
        squares = jnp.sum(g * g, axis=1, keepdims=True)
        part = dot((g * par[5:6]).astype(BF16), wo[...], ((1,), (0,))).astype(BF16)
        where = lax.broadcasted_iota(jnp.int32, (16, 128), 1)
        high = squares.astype(BF16).astype(F32)
        low = squares - high
        for h in range(2):
            at = 32 * h
            lines = [
                jnp.where(where % 64 < 32, high[at + 16 * e : at + 16 * e + 16], low[at + 16 * e : at + 16 * e + 16])
                for e in range(2)
            ]
            squares_tile = jnp.where(where < 64, lines[0], lines[1]).astype(BF16)
            chunk = 2 * d + h
            po_send[chunk, 0:32, :] = part[at : at + 32, 0:128]
            po_send[chunk, 32:64, :] = part[at : at + 32, 128:256]
            po_send[chunk, 64:80, :] = squares_tile

            @pl.when(chunk != r)
            def _():
                remote(po_send.at[chunk], po_recv.at[r], po_s.at[chunk], po_r.at[r], (f, chunk)).start()

            @pl.when(chunk == r)
            def _():
                po_recv[r] = po_send[r]

    project_out(f)

    @pl.loop(1, F)
    def _(o):
        s = source_of(f, o)
        remote(ga_all.at[s], ga_all.at[s], ga_s.at[s], ga_r.at[s], (f, r)).wait_recv()
        project_out(s)

    acc[0:32, 0:256] = jnp.zeros((32, 256), F32)

    @pl.loop(0, 4)
    def _(g):
        acc[32:64, 0:256] = jnp.zeros((32, 256), F32)
        ssum[...] = jnp.zeros((16, 128), F32)

        @pl.loop(0, 8)
        def _(i):
            s = 8 * g + i

            @pl.when(s != r)
            def _():
                remote(po_send.at[s], po_recv.at[s], po_s.at[s], po_r.at[s], (f, r)).wait_recv()

            acc[32:64, 0:128] += po_recv[s, 0:32, :].astype(F32)
            acc[32:64, 128:256] += po_recv[s, 32:64, :].astype(F32)
            ssum[...] += po_recv[s, 64:80, :].astype(F32)

        squares = ssum[...]
        squares = jnp.concatenate(
            [squares[:, 0:1] + squares[:, 32:33], squares[:, 64:65] + squares[:, 96:97]], axis=0
        )
        scale = lax.rsqrt(squares / (HPG * 128) + EPS)
        acc[0:32, 0:256] += acc[32:64, 0:256] * scale

    for k in range(2):
        fin_send[k] = acc[0:32, 128 * k : 128 * k + 128].astype(BF16)

        @pl.when(jnp.logical_not(is_self(k)))
        def _():
            remote(
                fin_send.at[k], fin_recv.at[half], fin_s.at[k], fin_r.at[half], (home, 2 * f + k)
            ).start()

        @pl.when(is_self(k))
        def _():
            fin_recv[k] = fin_send[k]

    for k in range(2):

        @pl.when(jnp.logical_not(is_self(k)))
        def _():
            remote(fin_send.at[k], fin_recv.at[k], fin_s.at[k], fin_r.at[k], (f, r)).wait_recv()

        out[32 * k : 32 * k + 32, :] = fin_recv[k]

    for k in range(2):

        @pl.when(jnp.logical_not(is_self(k)))
        def _():
            remote(hid.at[pl.ds(0, 32)], hid_all.at[r, k], h1_s.at[k], h1_r.at[k], (f, r)).wait_send()
            remote(fin_send.at[k], fin_recv.at[k], fin_s.at[k], fin_r.at[k], (f, r)).wait_send()

    @pl.loop(1, R)
    def _(o):
        to = (r + o) % R
        remote(hid_all.at[r], hid_all.at[r], h2_s.at[to], h2_r.at[r], (f, r)).wait_send()
        remote(po_send.at[to], po_recv.at[r], po_s.at[to], po_r.at[r], (f, r)).wait_send()

    @pl.loop(1, F)
    def _(o):
        d = peer_of(f, o)
        remote(winp.at[d], w_recv.at[f], w_s.at[d], w_r.at[f], (f, r)).wait_send()
        rows = pl.ds(2 * d, 2)
        remote(st_send.at[rows], st_recv.at[rows], st_s.at[d], st_r.at[f], (f, r)).wait_send()
        remote(p_send.at[d], p_recv.at[f], p_s.at[d], p_r.at[f], (f, r)).wait_send()
        remote(ga_all.at[f], ga_all.at[f], ga_s.at[d], ga_r.at[f], (f, r)).wait_send()

    @pl.loop(0, 8)
    def _(m):
        @pl.when(first_user + m != r)
        def _():
            remote(gc_send, gc_recv.at[piece], gc_s.at[m], gc_r.at[piece], (f, r)).wait_send()


def mixer(idx, hid, wi, wg, wgs, wo, par, winp, state):
    vmem = pl.BlockSpec(memory_space=pltpu.VMEM)
    dma = pltpu.SemaphoreType.DMA
    pairs = [2, R, F, F, F, 8, F, R, 2]
    return pl.pallas_call(
        kernel,
        out_shape=(
            jax.ShapeDtypeStruct((64, 128), BF16),
            jax.ShapeDtypeStruct((SLOTS, 256, 256), BF16),
            jax.ShapeDtypeStruct((48, 256), BF16),
            jax.ShapeDtypeStruct((48, 128), BF16),
        ),
        in_specs=[pl.BlockSpec(memory_space=pltpu.SMEM)] + [vmem] * 7 + [pl.BlockSpec(memory_space=pl.ANY)],
        out_specs=(vmem,) * 4,
        scratch_shapes=[
            pltpu.VMEM((R, 2, 32, 128), BF16),
            pltpu.VMEM((F, 64, 640), BF16),
            pltpu.VMEM((F, 64, 640), BF16),
            pltpu.VMEM((F, 16, 128), BF16),
            pltpu.VMEM((F, 16, 128), F32),
            pltpu.VMEM((SLOTS, 256, 256), BF16),
            pltpu.VMEM((2 * F, 256, 256), BF16),
            pltpu.VMEM((2 * F, 256, 256), BF16),
            pltpu.VMEM((64, 128), BF16),
            pltpu.VMEM((8, 64, 128), BF16),
            pltpu.VMEM((F, 64, 256), BF16),
            pltpu.VMEM((R, 80, 128), BF16),
            pltpu.VMEM((R, 80, 128), BF16),
            pltpu.VMEM((2, 32, 128), BF16),
            pltpu.VMEM((2, 32, 128), BF16),
            pltpu.VMEM((64, 640), F32),
            pltpu.VMEM((SLOTS, 8, 256), F32),
            pltpu.VMEM((SLOTS, 8, 256), F32),
            pltpu.VMEM((SLOTS, 8, 256), F32),
            pltpu.VMEM((SLOTS, 8, 256), F32),
            pltpu.VMEM((16, 128), F32),
            pltpu.SMEM((SLOTS,), jnp.int32),
        ]
        + [dma((n,)) for n in pairs for _ in range(2)]
        + [dma((1,))],
        compiler_params=pltpu.CompilerParams(
            collective_id=0, has_side_effects=True, vmem_limit_bytes=48 * 2**20
        ),
        name="mixer",
    )(idx, hid, wi, wg, wgs, wo, par, winp, state)


def on_device(
    hidden,
    inner_weight,
    gate_weight,
    group_weight,
    step_weight,
    output_weight,
    filter_inner,
    filter_inner_bias,
    filter_group,
    filter_group_bias,
    step_bias,
    decay_rate,
    skip_gain,
    norm_gain,
    recurrent_state,
    filter_inner_state,
    filter_group_state,
    live_counts,
    target_device,
    target_slot,
):
    slot = jnp.arange(SLOTS, dtype=jnp.int32)
    device = jnp.arange(F, dtype=jnp.int32)
    match = (slot < live_counts[0])[:, None] & (target_device[:, None] == device[None, :])
    earlier = jnp.sum(
        (match[:, None, :] & (slot[:, None] < slot[None, :])[:, :, None]).astype(jnp.int32), axis=0
    )
    chosen = match[:, :, None] & (earlier[:, :, None] == jnp.arange(2, dtype=jnp.int32))
    picker = chosen.reshape(SLOTS, 2 * F)
    idx = jnp.sum(jnp.where(picker, slot[:, None], 0), axis=0)
    sent_slot = jnp.sum(jnp.where(picker, target_slot[:, None] + 1, 0), axis=0) - 1
    flat = jnp.concatenate(
        [filter_inner_state.reshape(SLOTS, 768), filter_group_state.reshape(SLOTS, 192)], axis=1
    )
    packed = lax.dot_general(
        picker.astype(BF16), flat, (((0,), (0,)), ((), ())), preferred_element_type=F32
    ).astype(BF16)
    slot_columns = jnp.broadcast_to(sent_slot[:, None], (2 * F, 64)).astype(BF16)
    winp = jnp.concatenate([packed, slot_columns], axis=1).reshape(F, 16, 128)

    def head_row(values):
        return jnp.repeat(values, 128).reshape(1, 256)

    par = jnp.concatenate(
        [
            filter_inner,
            filter_inner_bias.reshape(1, 256),
            norm_gain.reshape(1, 256),
            head_row(skip_gain),
            head_row(step_bias),
            head_row(decay_rate),
            jnp.pad(filter_group, ((0, 0), (0, 192))),
            jnp.pad(filter_group_bias.reshape(1, 64), ((0, 0), (0, 192))),
            jnp.zeros((2, 256), F32),
        ],
        axis=0,
    )
    wgs = jnp.concatenate([group_weight, step_weight, jnp.zeros((256, 62), BF16)], axis=1)
    out, new_state, win_i, win_g = mixer(
        idx,
        hidden.reshape(64, 128),
        inner_weight,
        gate_weight,
        wgs,
        output_weight,
        par,
        winp,
        recurrent_state.reshape(SLOTS, 256, 256),
    )
    return (
        out.reshape(NSTEP, SLOTS, 128),
        new_state.reshape(SLOTS, 2, 128, 256),
        jnp.transpose(win_i.reshape(3, SLOTS, 256), (1, 0, 2)),
        jnp.transpose(win_g[:, 0:64].reshape(3, SLOTS, 64), (1, 0, 2)),
    )


def solution(mesh):
    return jax.shard_map(
        on_device,
        mesh=mesh,
        in_specs=(
            P(None, "fsdp", "roll"),
            P("fsdp", "roll"),
            P("fsdp", "roll"),
            P("fsdp", "roll"),
            P("fsdp", "roll"),
            P("roll", "fsdp"),
            P(None, "roll"),
            P("roll"),
            P(None, "roll"),
            P("roll"),
            P("roll"),
            P("roll"),
            P("roll"),
            P("roll"),
            P("fsdp", "roll", None, None),
            P("fsdp", None, "roll"),
            P("fsdp", None, "roll"),
            P("fsdp"),
            P("fsdp"),
            P("fsdp"),
        ),
        out_specs=(
            P(None, "fsdp", "roll"),
            P("fsdp", "roll", None, None),
            P("fsdp", None, "roll"),
            P("fsdp", None, "roll"),
        ),
        check_vma=False,
    )
```

```python
import jax
import jax.numpy as jnp
from jax import lax
from jax.experimental import pallas as pl
from jax.experimental.pallas import tpu as pltpu
from jax.sharding import PartitionSpec as P

MESH = pl.DeviceIdType.MESH
F = 16
R = 32
Z = 8
HPG = 16
NSTEP = 4
SLOTS = 16
EPS = 1e-05
EARLY = 4
F32 = jnp.float32
BF16 = jnp.bfloat16


def peer_of(f, o):
    return ((f // Z + o // Z) % 2) * Z + (f % Z + o % Z) % Z


def source_of(f, o):
    return ((f // Z + o // Z) % 2) * Z + (f % Z + Z - o % Z) % Z


def order(i):
    g, m = i // 4 + 1, i % 4
    near = (m // 2) * Z + jnp.where(m % 2 == 0, g, Z - g)
    return jnp.where(i < 12, near, jnp.where(i == 12, Z, 4 + Z * (i - 13)))


def silu(v):
    return v / (1.0 + jnp.exp(-v))


def dot(a, b, dims):
    return lax.dot_general(a, b, (dims, ((), ())), preferred_element_type=F32)


def kernel(
    live_h, td_h, ts_h, sb_h, dr_h, sg_h, hid_h, wi_h, wg_h, wgr_h, wst_h, wo_h, fi_h, fib_h, fg_h, fgb_h, gain_h,
    wini_h, wing_h, state,
    out, new_state, win_i, win_g,
    live, td, ts, sb, dr, sg, hid, wi, wg, wgr, wst, wo, fi, fib, fg, fgb, gain, wini, wing,
    wgs, gpar, win32, w_send, wg32,
    hid_all, p_send, p_recv, w_recv, w32, st_v, st_send, st_recv, gc_send, gc_recv,
    ga_all, po_send, po_recv, fin_send, fin_recv, acc, ck, bk, uk, yk, ssum, jq,
    h1_s, h1_r, h2_s, h2_r, w_s, w_r, st_s, st_r, p_s, p_r, gc_s, gc_r, ga_s, ga_r, po_s, po_r, fin_s, fin_r, loc,
):
    f = lax.axis_index("fsdp")
    r = lax.axis_index("roll")
    half = r % 2
    home = r // 2

    def remote(src, dst, s, d, device):
        return pltpu.make_async_remote_copy(
            src_ref=src, dst_ref=dst, send_sem=s, recv_sem=d, device_id=device, device_id_type=MESH
        )

    pairs = [
        (hid_h, hid), (td_h, td), (ts_h, ts), (live_h, live), (state, st_v), (wini_h, wini), (wing_h, wing),
        (wi_h, wi), (wg_h, wg), (wgr_h, wgr), (wst_h, wst), (fi_h, fi), (fib_h, fib), (fg_h, fg), (fgb_h, fgb),
        (sb_h, sb), (dr_h, dr), (sg_h, sg), (wo_h, wo), (gain_h, gain),
    ]
    loads = [pltpu.make_async_copy(a, b, loc.at[i]) for i, (a, b) in enumerate(pairs)]
    for load in loads:
        load.start()

    barrier = pltpu.get_barrier_semaphore()

    @pl.loop(1, F)
    def _(o):
        pl.semaphore_signal(barrier, inc=1, device_id=(peer_of(f, o), r), device_id_type=MESH)

    @pl.loop(1, R)
    def _(o):
        pl.semaphore_signal(barrier, inc=1, device_id=(f, (r + o) % R), device_id_type=MESH)

    def is_self(k):
        return (home == f) & (half == k)

    @pl.when(home != f)
    def _():
        for k in range(2):
            pl.semaphore_signal(barrier, inc=1, device_id=(home, 2 * f + k), device_id_type=MESH)

    for load in loads[1:4] + loads[5:15]:
        load.wait()
    wgs[...] = jnp.zeros((128, 256), BF16)
    wgs[0:64, :] = wgr[...]
    wgs[64:66, :] = wst[...]
    gpar[...] = jnp.zeros((8, 128), F32)
    gpar[0:4, 0:64] = fg[...]
    gpar[4:5, 0:64] = fgb[...]
    for k in range(3):
        win32[:, 2 * k, :] = wini[k, :, 0:128].astype(F32)
        win32[:, 2 * k + 1, :] = wini[k, :, 128:256].astype(F32)
    wg32[...] = jnp.zeros((3, SLOTS, 128), F32)
    for k in range(3):
        wg32[k, :, 0:64] = wing[k].astype(F32)
    win32[:, 6, :] = wg32[0] + pltpu.roll(wg32[1], 64, 1)
    win32[:, 7, :] = wg32[2]

    def picks(d):
        count = jnp.int32(0)
        got = [jnp.int32(0), jnp.int32(0)]
        to = [jnp.int32(-1), jnp.int32(-1)]
        for i in range(SLOTS):
            hit = (i < live[0]) & (td[i] == d)
            for c in range(2):
                mine = hit & (count == c)
                got[c] = jnp.where(mine, i, got[c])
                to[c] = jnp.where(mine, ts[i], to[c])
            count = count + jnp.where(hit, 1, 0)
        return got, to

    row8 = lax.broadcasted_iota(jnp.int32, (8, 128), 0)
    lane8 = lax.broadcasted_iota(jnp.int32, (8, 128), 1)

    @pl.loop(0, F)
    def _(d):
        got, to = picks(d)
        w_send[d] = jnp.concatenate(
            [
                jnp.where((row8 == 7) & (lane8 >= 64), to[c].astype(F32), win32[got[c]])
                for c in range(2)
            ],
            axis=0,
        ).astype(BF16)

    loads[0].wait()
    pl.semaphore_wait(barrier, F - 1 + R - 1 + jnp.where(home != f, 2, 0))

    for k in range(2):

        @pl.when(jnp.logical_not(is_self(k)))
        def _():
            remote(
                hid.at[pl.ds(32 * k, 32)], hid_all.at[2 * f + k, half], h1_s.at[k], h1_r.at[half],
                (home, 2 * f + k),
            ).start()

        @pl.when(is_self(k))
        def _():
            hid_all[r, k] = hid[pl.ds(32 * k, 32), :]

    @pl.loop(0, F - 1)
    def _(i):
        d = peer_of(f, order(i))
        remote(w_send.at[d], w_recv.at[f], w_s.at[d], w_r.at[f], (d, r)).start()

    w_recv[f] = w_send[f]

    loads[4].wait()

    def send_states(i):
        d = peer_of(f, order(i))
        got, _ = picks(d)
        for c in range(2):
            st_send[2 * d + c] = st_v[got[c]]
        remote(
            st_send.at[pl.ds(2 * d, 2)], st_recv.at[pl.ds(2 * f, 2)], st_s.at[d], st_r.at[f], (d, r)
        ).start()

    @pl.loop(0, EARLY)
    def _(i):
        send_states(i)

    for k in range(2):

        @pl.when(jnp.logical_not(is_self(k)))
        def _():
            remote(hid.at[pl.ds(0, 32)], hid_all.at[r, k], h1_s.at[k], h1_r.at[k], (f, r)).wait_recv()

    @pl.loop(1, R)
    def _(o):
        to = (r + o) % R
        remote(hid_all.at[r], hid_all.at[r], h2_s.at[to], h2_r.at[r], (f, to)).start()

    @pl.loop(EARLY, F - 1)
    def _(i):
        send_states(i)

    got, _ = picks(f)
    for c in range(2):
        st_recv[2 * f + c] = st_v[got[c]]

    def project(d):
        for h in range(2):
            chunk = 2 * d + h

            @pl.when(chunk != r)
            def _():
                remote(
                    hid_all.at[chunk], hid_all.at[chunk], h2_s.at[chunk], h2_r.at[chunk], (f, r)
                ).wait_recv()

        rows = jnp.concatenate(
            [
                jnp.concatenate([hid_all[2 * d + h, 0], hid_all[2 * d + h, 1]], axis=1)
                for h in range(2)
            ],
            axis=0,
        )
        nn = ((1,), (0,))
        return (
            dot(rows, wi[...], nn).astype(BF16),
            dot(rows, wg[...], nn).astype(BF16),
            dot(rows, wgs[...], ((1,), (1,))).astype(BF16),
        )

    @pl.loop(0, F - 1)
    def _(i):
        d = peer_of(f, order(i))
        a, b, c = project(d)
        p_send[d, :, 0:256] = a
        p_send[d, :, 256:512] = b
        p_send[d, :, 512:640] = c
        remote(p_send.at[d], p_recv.at[f], p_s.at[d], p_r.at[f], (d, r)).start()

    a, b, c = project(f)
    acc[:, 0:256] = a.astype(F32)
    acc[:, 256:512] = b.astype(F32)
    acc[:, 512:640] = c.astype(F32)

    @pl.loop(1, F)
    def _(o):
        s = source_of(f, o)
        remote(w_send.at[s], w_recv.at[s], w_s.at[s], w_r.at[s], (f, r)).wait_recv()

    w32[...] = w_recv[...].astype(F32)
    lane = lax.broadcasted_iota(jnp.int32, (F, 128), 1)
    row = lax.broadcasted_iota(jnp.int32, (F, 128), 0)
    placers = []
    code = jnp.zeros((F, 128), F32)
    for c in range(2):
        slot = w32[:, 8 * c + 7, :][:, 64:65].astype(jnp.int32)
        hit = slot == lane
        placers.append(hit.astype(F32).astype(BF16))
        code = code + jnp.where(hit, (2 * row + c + 1).astype(F32), 0.0)

    @pl.loop(0, SLOTS)
    def _(q):
        jq[q] = jnp.sum(jnp.where(lane == q, code, 0.0)).astype(jnp.int32) - 1

    moved = []
    for block in range(8):
        total = jnp.zeros((128, 128), F32)
        for c in range(2):
            total = total + dot(placers[c], w32[:, 8 * c + block, :].astype(BF16), ((0,), (0,)))
        moved.append(total[0:SLOTS])
    prior_i = [jnp.concatenate([moved[2 * k], moved[2 * k + 1]], axis=1) for k in range(3)]
    prior_g = [moved[6], pltpu.roll(moved[6], 64, 1), moved[7]]

    @pl.loop(0, F - 1)
    def _(i):
        s = source_of(f, order(i))
        remote(p_send.at[s], p_recv.at[s], p_s.at[s], p_r.at[s], (f, r)).wait_recv()
        acc[...] += p_recv[s].astype(F32)

    raw = acc[...].astype(BF16)
    raw = raw.astype(F32)
    for t in range(1, NSTEP):
        rows = slice(SLOTS * t, SLOTS * (t + 1))
        win_i[t - 1] = raw[rows, 0:256].astype(BF16)
        win_g[t - 1] = raw[rows, 512:576].astype(BF16)

    def conv(prior, fresh, taps, bias):
        steps = prior + [fresh[SLOTS * t : SLOTS * (t + 1)] for t in range(NSTEP)]
        got = []
        for t in range(NSTEP):
            total = bias
            for k in range(4):
                total = total + taps[k] * steps[t + k]
            got.append(silu(total))
        return got

    group = jnp.concatenate(
        conv(prior_g, raw[:, 512:640], [gpar[k : k + 1] for k in range(4)], gpar[4:5]),
        axis=0,
    )
    gc_send[...] = jnp.where(half == 1, pltpu.roll(group, 64, 1), group).astype(BF16)
    piece = (r // 16) * 4 + r % 4
    first_user = 8 * ((r % 16) // 4)

    @pl.loop(0, 8)
    def _(m):
        to = first_user + m

        @pl.when(to != r)
        def _():
            remote(gc_send, gc_recv.at[piece], gc_s.at[m], gc_r.at[piece], (f, to)).start()

        @pl.when(to == r)
        def _():
            gc_recv[piece] = gc_send[...]

    xs = conv(prior_i, raw[:, 0:256], [fi[k : k + 1] for k in range(4)], fib[...])
    step_raw = jnp.concatenate(
        [
            jnp.broadcast_to(raw[:, 576:577], (NSTEP * SLOTS, 128)),
            jnp.broadcast_to(raw[:, 577:578], (NSTEP * SLOTS, 128)),
        ],
        axis=1,
    )
    for load in loads[15:]:
        load.wait()

    def head_row(values):
        return jnp.where(lax.broadcasted_iota(jnp.int32, (1, 256), 1) < 128, values[0], values[1])

    v = step_raw + head_row(sb)
    dt = jnp.maximum(v, 0.0) + jnp.log1p(jnp.exp(-jnp.abs(v)))
    dec = jnp.exp(-dt * head_row(dr))
    dts = [dt[SLOTS * t : SLOTS * (t + 1)] for t in range(NSTEP)]
    decs = [dec[SLOTS * t : SLOTS * (t + 1)] for t in range(NSTEP)]

    @pl.loop(0, 8)
    def _(i):
        s = (i // 4) * 16 + 4 * (r // 8) + i % 4

        @pl.when(s != r)
        def _():
            remote(gc_send, gc_recv.at[i], gc_s.at[i], gc_r.at[i], (f, r)).wait_recv()

    def basis(i):
        return jnp.concatenate(
            [
                gc_recv[i].astype(F32) + gc_recv[i + 1].astype(F32),
                gc_recv[i + 2].astype(F32) + gc_recv[i + 3].astype(F32),
            ],
            axis=1,
        )

    b_all, c_all = basis(0), basis(4)
    bs = [b_all[SLOTS * t : SLOTS * (t + 1)] for t in range(NSTEP)]
    cs = [c_all[SLOTS * t : SLOTS * (t + 1)] for t in range(NSTEP)]
    us = [dts[t] * xs[t] for t in range(NSTEP)]
    ck[...] = jnp.zeros(ck.shape, F32)
    bk[...] = jnp.zeros(bk.shape, F32)
    uk[...] = jnp.zeros(uk.shape, F32)
    for t in range(NSTEP):
        ck[:, t, :] = cs[t]
        bk[:, t, :] = bs[t]
    tail = None
    for t in reversed(range(NSTEP)):
        uk[:, t, :] = us[t] if tail is None else us[t] * tail
        tail = decs[t] if tail is None else decs[t] * tail
    uk[:, 4, :] = tail

    @pl.loop(1, F)
    def _(o):
        s = source_of(f, o)
        rows = pl.ds(2 * s, 2)
        remote(st_send.at[rows], st_recv.at[rows], st_s.at[s], st_r.at[s], (f, r)).wait_recv()

    @pl.loop(0, SLOTS)
    def _(q):
        j = jq[q]
        start = st_recv[jnp.clip(j, 0, 2 * F - 1)]
        y = dot(ck[q].astype(BF16), start, ((1,), (1,)))
        yk[q] = jnp.where(j >= 0, y, 0.0)

    gates = silu(raw[:, 256:512])
    gated = []
    for t in range(NSTEP):
        total = None
        grown = None
        for s in reversed(range(t + 1)):
            pair = jnp.sum(bs[s] * cs[t], axis=1, keepdims=True)
            term = us[s] * pair
            if grown is not None:
                term = term * grown
            total = term if total is None else total + term
            grown = decs[s] if grown is None else grown * decs[s]
        total = total + grown * yk[:, t, :] + head_row(sg) * xs[t]
        gated.append(total * gates[SLOTS * t : SLOTS * (t + 1)])
    ga_all[f] = jnp.concatenate(gated, axis=0).astype(BF16)

    @pl.loop(0, F - 1)
    def _(i):
        d = peer_of(f, order(i))
        remote(ga_all.at[f], ga_all.at[f], ga_s.at[d], ga_r.at[f], (d, r)).start()

    @pl.loop(0, SLOTS)
    def _(q):
        j = jq[q]
        start = st_recv[jnp.clip(j, 0, 2 * F - 1)].astype(F32)
        start = jnp.where(j >= 0, start, 0.0)
        u = uk[q]
        rate = u[4:5]
        keep = lax.broadcasted_iota(jnp.int32, (8, 256), 0) < 4
        u = jnp.where(keep, u, 0.0)
        high = u.astype(BF16)
        low = (u - high.astype(F32)).astype(BF16)
        b = bk[q].astype(BF16)
        added = dot(
            jnp.concatenate([high, low], axis=0), jnp.concatenate([b, b], axis=0), ((0,), (0,))
        )
        for h in range(2):
            rows = slice(128 * h, 128 * h + 128)
            factor = jnp.concatenate([rate[:, rows], rate[:, rows]], axis=1)
            new_state[q, rows, :] = (start[rows] * factor + added[rows]).astype(BF16)

    def project_out(d):
        g = ga_all[d].astype(F32)
        squares = jnp.sum(g * g, axis=1, keepdims=True)
        part = dot((g * gain[...]).astype(BF16), wo[...], ((1,), (0,))).astype(BF16)
        where = lax.broadcasted_iota(jnp.int32, (16, 128), 1)
        high = squares.astype(BF16).astype(F32)
        low = squares - high
        for h in range(2):
            at = 32 * h
            lines = [
                jnp.where(where % 64 < 32, high[at + 16 * e : at + 16 * e + 16], low[at + 16 * e : at + 16 * e + 16])
                for e in range(2)
            ]
            squares_tile = jnp.where(where < 64, lines[0], lines[1]).astype(BF16)
            chunk = 2 * d + h
            po_send[chunk, 0:32, :] = part[at : at + 32, 0:128]
            po_send[chunk, 32:64, :] = part[at : at + 32, 128:256]
            po_send[chunk, 64:80, :] = squares_tile

            @pl.when(chunk != r)
            def _():
                remote(po_send.at[chunk], po_recv.at[r], po_s.at[chunk], po_r.at[r], (f, chunk)).start()

            @pl.when(chunk == r)
            def _():
                po_recv[r] = po_send[r]

    project_out(f)

    @pl.loop(0, F - 1)
    def _(i):
        s = source_of(f, order(i))
        remote(ga_all.at[s], ga_all.at[s], ga_s.at[s], ga_r.at[s], (f, r)).wait_recv()
        project_out(s)

    acc[0:32, 0:256] = jnp.zeros((32, 256), F32)

    @pl.loop(0, 4)
    def _(g):
        acc[32:64, 0:256] = jnp.zeros((32, 256), F32)
        ssum[...] = jnp.zeros((16, 128), F32)

        @pl.loop(0, 8)
        def _(i):
            s = 8 * g + i

            @pl.when(s != r)
            def _():
                remote(po_send.at[s], po_recv.at[s], po_s.at[s], po_r.at[s], (f, r)).wait_recv()

            acc[32:64, 0:128] += po_recv[s, 0:32, :].astype(F32)
            acc[32:64, 128:256] += po_recv[s, 32:64, :].astype(F32)
            ssum[...] += po_recv[s, 64:80, :].astype(F32)

        squares = ssum[...]
        squares = jnp.concatenate(
            [squares[:, 0:1] + squares[:, 32:33], squares[:, 64:65] + squares[:, 96:97]], axis=0
        )
        scale = lax.rsqrt(squares / (HPG * 128) + EPS)
        acc[0:32, 0:256] += acc[32:64, 0:256] * scale

    for k in range(2):
        fin_send[k] = acc[0:32, 128 * k : 128 * k + 128].astype(BF16)

        @pl.when(jnp.logical_not(is_self(k)))
        def _():
            remote(
                fin_send.at[k], fin_recv.at[half], fin_s.at[k], fin_r.at[half], (home, 2 * f + k)
            ).start()

        @pl.when(is_self(k))
        def _():
            fin_recv[k] = fin_send[k]

    for k in range(2):

        @pl.when(jnp.logical_not(is_self(k)))
        def _():
            remote(fin_send.at[k], fin_recv.at[k], fin_s.at[k], fin_r.at[k], (f, r)).wait_recv()

        out[32 * k : 32 * k + 32, :] = fin_recv[k]

    for k in range(2):

        @pl.when(jnp.logical_not(is_self(k)))
        def _():
            remote(hid.at[pl.ds(0, 32)], hid_all.at[r, k], h1_s.at[k], h1_r.at[k], (f, r)).wait_send()
            remote(fin_send.at[k], fin_recv.at[k], fin_s.at[k], fin_r.at[k], (f, r)).wait_send()

    @pl.loop(1, R)
    def _(o):
        to = (r + o) % R
        remote(hid_all.at[r], hid_all.at[r], h2_s.at[to], h2_r.at[r], (f, r)).wait_send()
        remote(po_send.at[to], po_recv.at[r], po_s.at[to], po_r.at[r], (f, r)).wait_send()

    @pl.loop(1, F)
    def _(o):
        d = peer_of(f, o)
        remote(w_send.at[d], w_recv.at[f], w_s.at[d], w_r.at[f], (f, r)).wait_send()
        rows = pl.ds(2 * d, 2)
        remote(st_send.at[rows], st_recv.at[rows], st_s.at[d], st_r.at[f], (f, r)).wait_send()
        remote(p_send.at[d], p_recv.at[f], p_s.at[d], p_r.at[f], (f, r)).wait_send()
        remote(ga_all.at[f], ga_all.at[f], ga_s.at[d], ga_r.at[f], (f, r)).wait_send()

    @pl.loop(0, 8)
    def _(m):
        @pl.when(first_user + m != r)
        def _():
            remote(gc_send, gc_recv.at[piece], gc_s.at[m], gc_r.at[piece], (f, r)).wait_send()


def mixer(*operands):
    vmem = pl.BlockSpec(memory_space=pltpu.VMEM)
    dma = pltpu.SemaphoreType.DMA
    pairs = [2, R, F, F, F, 8, F, R, 2]
    held = [(pltpu.SMEM if x.ndim == 1 else pltpu.VMEM)(x.shape, x.dtype) for x in operands[:-1]]
    return pl.pallas_call(
        kernel,
        out_shape=(
            jax.ShapeDtypeStruct((64, 128), BF16),
            jax.ShapeDtypeStruct((SLOTS, 256, 256), BF16),
            jax.ShapeDtypeStruct((3, SLOTS, 256), BF16),
            jax.ShapeDtypeStruct((3, SLOTS, 64), BF16),
        ),
        in_specs=[pl.BlockSpec(memory_space=pl.ANY)] * len(operands),
        out_specs=(vmem,) * 4,
        scratch_shapes=held
        + [
            pltpu.VMEM((128, 256), BF16),
            pltpu.VMEM((8, 128), F32),
            pltpu.VMEM((SLOTS, 8, 128), F32),
            pltpu.VMEM((F, 16, 128), BF16),
            pltpu.VMEM((3, SLOTS, 128), F32),
            pltpu.VMEM((R, 2, 32, 128), BF16),
            pltpu.VMEM((F, 64, 640), BF16),
            pltpu.VMEM((F, 64, 640), BF16),
            pltpu.VMEM((F, 16, 128), BF16),
            pltpu.VMEM((F, 16, 128), F32),
            pltpu.VMEM((SLOTS, 256, 256), BF16),
            pltpu.VMEM((2 * F, 256, 256), BF16),
            pltpu.VMEM((2 * F, 256, 256), BF16),
            pltpu.VMEM((64, 128), BF16),
            pltpu.VMEM((8, 64, 128), BF16),
            pltpu.VMEM((F, 64, 256), BF16),
            pltpu.VMEM((R, 80, 128), BF16),
            pltpu.VMEM((R, 80, 128), BF16),
            pltpu.VMEM((2, 32, 128), BF16),
            pltpu.VMEM((2, 32, 128), BF16),
            pltpu.VMEM((64, 640), F32),
            pltpu.VMEM((SLOTS, 8, 256), F32),
            pltpu.VMEM((SLOTS, 8, 256), F32),
            pltpu.VMEM((SLOTS, 8, 256), F32),
            pltpu.VMEM((SLOTS, 8, 256), F32),
            pltpu.VMEM((16, 128), F32),
            pltpu.SMEM((SLOTS,), jnp.int32),
        ]
        + [dma((n,)) for n in pairs for _ in range(2)]
        + [dma((len(operands),))],
        compiler_params=pltpu.CompilerParams(
            collective_id=0, has_side_effects=True, vmem_limit_bytes=60 * 2**20
        ),
        name="mixer",
    )(*operands)


def on_device(
    hidden,
    inner_weight,
    gate_weight,
    group_weight,
    step_weight,
    output_weight,
    filter_inner,
    filter_inner_bias,
    filter_group,
    filter_group_bias,
    step_bias,
    decay_rate,
    skip_gain,
    norm_gain,
    recurrent_state,
    filter_inner_state,
    filter_group_state,
    live_counts,
    target_device,
    target_slot,
):
    out, new_state, win_i, win_g = mixer(
        live_counts,
        target_device,
        target_slot,
        step_bias,
        decay_rate,
        skip_gain,
        hidden.reshape(64, 128),
        inner_weight,
        gate_weight,
        group_weight.T,
        step_weight.T,
        output_weight,
        filter_inner,
        filter_inner_bias.reshape(1, 256),
        filter_group,
        filter_group_bias.reshape(1, 64),
        norm_gain.reshape(1, 256),
        jnp.transpose(filter_inner_state, (1, 0, 2)),
        jnp.transpose(filter_group_state, (1, 0, 2)),
        recurrent_state.reshape(SLOTS, 256, 256),
    )
    return (
        out.reshape(NSTEP, SLOTS, 128),
        new_state.reshape(SLOTS, 2, 128, 256),
        jnp.transpose(win_i, (1, 0, 2)),
        jnp.transpose(win_g, (1, 0, 2)),
    )


def solution(mesh):
    return jax.shard_map(
        on_device,
        mesh=mesh,
        in_specs=(
            P(None, "fsdp", "roll"),
            P("fsdp", "roll"),
            P("fsdp", "roll"),
            P("fsdp", "roll"),
            P("fsdp", "roll"),
            P("roll", "fsdp"),
            P(None, "roll"),
            P("roll"),
            P(None, "roll"),
            P("roll"),
            P("roll"),
            P("roll"),
            P("roll"),
            P("roll"),
            P("fsdp", "roll", None, None),
            P("fsdp", None, "roll"),
            P("fsdp", None, "roll"),
            P("fsdp"),
            P("fsdp"),
            P("fsdp"),
        ),
        out_specs=(
            P(None, "fsdp", "roll"),
            P("fsdp", "roll", None, None),
            P("fsdp", None, "roll"),
            P("fsdp", None, "roll"),
        ),
        check_vma=False,
    )
```

```python
import jax
import jax.numpy as jnp
from jax import lax
from jax.experimental import pallas as pl
from jax.experimental.pallas import tpu as pltpu
from jax.sharding import PartitionSpec as P

MESH = pl.DeviceIdType.MESH
F = 16
R = 32
Z = 8
HPG = 16
NSTEP = 4
SLOTS = 16
EPS = 1e-05
ALONG = (1, 7, 2, 6, 3, 5, 4)
ACROSS = (4, 3, 5, 2, 6, 1, 7, 0)
CROSS_ROWS = (0, 16, 0)
ALONG_ROWS = (0, 14, 0)
PASS_ROWS = (0, 14, 0)
F32 = jnp.float32
BF16 = jnp.bfloat16


def peer_of(f, o):
    return ((f // Z + o // Z) % 2) * Z + (f % Z + o % Z) % Z


def source_of(f, o):
    return ((f // Z + o // Z) % 2) * Z + (f % Z + Z - o % Z) % Z


def order(i):
    g, m = i // 4 + 1, i % 4
    near = (m // 2) * Z + jnp.where(m % 2 == 0, g, Z - g)
    return jnp.where(i < 12, near, jnp.where(i == 12, Z, 4 + Z * (i - 13)))


def silu(v):
    return v / (1.0 + jnp.exp(-v))


def dot(a, b, dims):
    return lax.dot_general(a, b, (dims, ((), ())), preferred_element_type=F32)


def kernel(
    live_h, td_h, ts_h, sb_h, dr_h, sg_h, hid_h, wi_h, wg_h, wgr_h, wst_h, wo_h, fi_h, fib_h, fg_h, fgb_h, gain_h,
    wini_h, wing_h, state,
    out, new_state, win_i, win_g,
    live, td, ts, sb, dr, sg, hid, wi, wg, wgr, wst, wo, fi, fib, fg, fgb, gain, wini, wing,
    wgs, gpar, win32, w_send, wg32,
    hid_all, p_send, p_recv, w_recv, w32, st_v, st_send, st_recv, gc_send, gc_recv,
    ga_all, po_send, po_recv, fin_send, fin_recv, acc, ck, bk, uk, yk, ssum, jq, pick, relay, py_send, py_recv,
    h1_s, h1_r, h2_s, h2_r, w_s, w_r, st_s, st_r, p_s, p_r, gc_s, gc_r, ga_s, ga_r, po_s, po_r, fin_s, fin_r, rl_s, rl_r, py_s, py_r, gf_s, gf_r, loc,
):
    f = lax.axis_index("fsdp")
    r = lax.axis_index("roll")
    half = r % 2
    home = r // 2

    def remote(src, dst, s, d, device):
        return pltpu.make_async_remote_copy(
            src_ref=src, dst_ref=dst, send_sem=s, recv_sem=d, device_id=device, device_id_type=MESH
        )

    pairs = [
        (hid_h, hid), (td_h, td), (ts_h, ts), (live_h, live), (state, st_v), (wini_h, wini), (wing_h, wing),
        (wi_h, wi), (wg_h, wg), (wgr_h, wgr), (wst_h, wst), (fi_h, fi), (fib_h, fib), (fg_h, fg), (fgb_h, fgb),
        (sb_h, sb), (dr_h, dr), (sg_h, sg), (wo_h, wo), (gain_h, gain),
    ]
    loads = [pltpu.make_async_copy(a, b, loc.at[i]) for i, (a, b) in enumerate(pairs)]
    for load in loads:
        load.start()

    barrier = pltpu.get_barrier_semaphore()

    @pl.loop(1, F)
    def _(o):
        pl.semaphore_signal(barrier, inc=1, device_id=(peer_of(f, o), r), device_id_type=MESH)

    @pl.loop(1, R)
    def _(o):
        pl.semaphore_signal(barrier, inc=1, device_id=(f, (r + o) % R), device_id_type=MESH)

    def is_self(k):
        return (home == f) & (half == k)

    @pl.when(home != f)
    def _():
        for k in range(2):
            pl.semaphore_signal(barrier, inc=1, device_id=(home, 2 * f + k), device_id_type=MESH)

    for load in loads[1:4] + loads[5:15]:
        load.wait()
    wgs[...] = jnp.zeros((128, 256), BF16)
    wgs[0:64, :] = wgr[...]
    wgs[64:66, :] = wst[...]
    gpar[...] = jnp.zeros((8, 128), F32)
    gpar[0:4, 0:64] = fg[...]
    gpar[4:5, 0:64] = fgb[...]
    for k in range(3):
        win32[:, 2 * k, :] = wini[k, :, 0:128].astype(F32)
        win32[:, 2 * k + 1, :] = wini[k, :, 128:256].astype(F32)
    wg32[...] = jnp.zeros((3, SLOTS, 128), F32)
    for k in range(3):
        wg32[k, :, 0:64] = wing[k].astype(F32)
    win32[:, 6, :] = wg32[0] + pltpu.roll(wg32[1], 64, 1)
    win32[:, 7, :] = wg32[2]

    def picks(d):
        count = jnp.int32(0)
        got = [jnp.int32(0), jnp.int32(0)]
        to = [jnp.int32(-1), jnp.int32(-1)]
        for i in range(SLOTS):
            hit = (i < live[0]) & (td[i] == d)
            for c in range(2):
                mine = hit & (count == c)
                got[c] = jnp.where(mine, i, got[c])
                to[c] = jnp.where(mine, ts[i], to[c])
            count = count + jnp.where(hit, 1, 0)
        return got, to

    row8 = lax.broadcasted_iota(jnp.int32, (8, 128), 0)
    lane8 = lax.broadcasted_iota(jnp.int32, (8, 128), 1)

    @pl.loop(0, F)
    def _(d):
        got, to = picks(d)
        for c in range(2):
            pick[2 * d + c] = got[c]
        w_send[d] = jnp.concatenate(
            [
                jnp.where((row8 == 7) & (lane8 >= 64), to[c].astype(F32), win32[got[c]])
                for c in range(2)
            ],
            axis=0,
        ).astype(BF16)

    loads[4].wait()

    @pl.loop(0, 2 * F)
    def _(j):
        st_send[j] = st_v[pick[j]]

    for c in range(2):
        st_recv[2 * f + c] = st_send[2 * f + c]

    fy, fz = f // Z, f % Z
    over = (1 - fy) * Z + fz

    def turn(b):
        return (fz + jnp.where(half == 0, b, (Z - b) % Z)) % Z

    def upto(rows, point):
        return range(sum(rows[:point]), sum(rows[: point + 1]))

    def send_rows(point):
        for k in upto(CROSS_ROWS, point):
            c = k % 2
            z = turn(ACROSS[k // 2])
            at = 2 * ((1 - fy) * Z + z) + c
            if ACROSS[k // 2]:
                remote(st_send.at[at], relay.at[2 * z + c], st_s.at[at], rl_r.at[2 * z + c], (over, r)).start()
            else:
                remote(st_send.at[at], st_recv.at[2 * f + c], st_s.at[at], st_r.at[2 * f + c], (over, r)).start()
        for k in upto(ALONG_ROWS, point):
            d = fy * Z + turn(ALONG[k // 2])
            at, to = 2 * d + k % 2, 2 * f + k % 2
            remote(st_send.at[at], st_recv.at[to], st_s.at[at], st_r.at[to], (d, r)).start()
        for k in upto(PASS_ROWS, point):
            z = turn(ACROSS[k // 2])
            at, to = 2 * z + k % 2, 2 * over + k % 2
            remote(relay.at[at], relay.at[at], rl_s.at[at], rl_r.at[at], (f, r)).wait_recv()
            remote(relay.at[at], st_recv.at[to], rl_s.at[at], st_r.at[to], (fy * Z + z, r)).start()

    loads[0].wait()
    pl.semaphore_wait(barrier, F - 1 + R - 1 + jnp.where(home != f, 2, 0))

    for k in range(2):

        @pl.when(jnp.logical_not(is_self(k)))
        def _():
            remote(
                hid.at[pl.ds(32 * k, 32)], hid_all.at[2 * f + k, half], h1_s.at[k], h1_r.at[half],
                (home, 2 * f + k),
            ).start()

        @pl.when(is_self(k))
        def _():
            hid_all[r, k] = hid[pl.ds(32 * k, 32), :]

    @pl.loop(0, F - 1)
    def _(i):
        d = peer_of(f, order(i))
        remote(w_send.at[d], w_recv.at[f], w_s.at[d], w_r.at[f], (d, r)).start()

    w_recv[f] = w_send[f]

    send_rows(0)

    for k in range(2):

        @pl.when(jnp.logical_not(is_self(k)))
        def _():
            remote(hid.at[pl.ds(0, 32)], hid_all.at[r, k], h1_s.at[k], h1_r.at[k], (f, r)).wait_recv()

    @pl.loop(1, R)
    def _(o):
        to = (r + o) % R
        remote(hid_all.at[r], hid_all.at[r], h2_s.at[to], h2_r.at[r], (f, to)).start()

    send_rows(1)

    def project(z):
        chunks = [2 * (y * Z + z) + h for y in range(2) for h in range(2)]
        for chunk in chunks:

            @pl.when(chunk != r)
            def _():
                remote(
                    hid_all.at[chunk], hid_all.at[chunk], h2_s.at[chunk], h2_r.at[chunk], (f, r)
                ).wait_recv()

        rows = jnp.concatenate(
            [jnp.concatenate([hid_all[chunk, 0], hid_all[chunk, 1]], axis=1) for chunk in chunks],
            axis=0,
        )
        nn = ((1,), (0,))
        return (
            dot(rows, wi[...], nn),
            dot(rows, wg[...], nn),
            dot(rows, wgs[...], ((1,), (1,))),
        )

    def along(i):
        return (fz + jnp.where(i % 2 == half, i // 2 + 1, Z - 1 - i // 2)) % Z

    @pl.loop(0, Z - 1)
    def _(i):
        z = along(i)
        parts = project(z)
        for y in range(2):
            rows = slice(64 * y, 64 * y + 64)
            p_send[z, y, :, 0:256] = parts[0][rows].astype(BF16)
            p_send[z, y, :, 256:512] = parts[1][rows].astype(BF16)
            p_send[z, y, :, 512:640] = parts[2][rows].astype(BF16)
        remote(p_send.at[z], p_recv.at[fz], p_s.at[z], p_r.at[fz], (fy * Z + z, r)).start()

    send_rows(2)
    parts = project(fz)
    for y in range(2):
        rows = slice(64 * y, 64 * y + 64)
        acc[y, :, 0:256] = parts[0][rows]
        acc[y, :, 256:512] = parts[1][rows]
        acc[y, :, 512:640] = parts[2][rows]

    @pl.loop(1, F)
    def _(o):
        s = source_of(f, o)
        remote(w_send.at[s], w_recv.at[s], w_s.at[s], w_r.at[s], (f, r)).wait_recv()

    w32[...] = w_recv[...].astype(F32)
    lane = lax.broadcasted_iota(jnp.int32, (F, 128), 1)
    row = lax.broadcasted_iota(jnp.int32, (F, 128), 0)
    placers = []
    code = jnp.zeros((F, 128), F32)
    for c in range(2):
        slot = w32[:, 8 * c + 7, :][:, 64:65].astype(jnp.int32)
        hit = slot == lane
        placers.append(hit.astype(F32).astype(BF16))
        code = code + jnp.where(hit, (2 * row + c + 1).astype(F32), 0.0)

    @pl.loop(0, SLOTS)
    def _(q):
        jq[q] = jnp.sum(jnp.where(lane == q, code, 0.0)).astype(jnp.int32) - 1

    moved = []
    for block in range(8):
        total = jnp.zeros((128, 128), F32)
        for c in range(2):
            total = total + dot(placers[c], w32[:, 8 * c + block, :].astype(BF16), ((0,), (0,)))
        moved.append(total[0:SLOTS])
    prior_i = [jnp.concatenate([moved[2 * k], moved[2 * k + 1]], axis=1) for k in range(3)]
    prior_g = [moved[6], pltpu.roll(moved[6], 64, 1), moved[7]]

    @pl.loop(0, Z - 1)
    def _(i):
        z = along(i)
        remote(p_send.at[z], p_recv.at[z], p_s.at[z], p_r.at[z], (f, r)).wait_recv()
        acc[1 - fy] += p_recv[z, 1 - fy].astype(F32)

    py_send[...] = acc[1 - fy].astype(BF16)
    across = remote(py_send, py_recv, py_s.at[0], py_r.at[0], (over, r))
    across.start()

    @pl.loop(0, Z - 1)
    def _(i):
        acc[fy] += p_recv[along(i), fy].astype(F32)

    across.wait_recv()
    raw = (acc[fy] + py_recv[...].astype(F32)).astype(BF16)
    raw = raw.astype(F32)
    for t in range(1, NSTEP):
        rows = slice(SLOTS * t, SLOTS * (t + 1))
        win_i[t - 1] = raw[rows, 0:256].astype(BF16)
        win_g[t - 1] = raw[rows, 512:576].astype(BF16)

    def conv(prior, fresh, taps, bias):
        steps = prior + [fresh[SLOTS * t : SLOTS * (t + 1)] for t in range(NSTEP)]
        got = []
        for t in range(NSTEP):
            total = bias
            for k in range(4):
                total = total + taps[k] * steps[t + k]
            got.append(silu(total))
        return got

    group = jnp.concatenate(
        conv(prior_g, raw[:, 512:640], [gpar[k : k + 1] for k in range(4)], gpar[4:5]),
        axis=0,
    )
    gc_send[...] = jnp.where(half == 1, pltpu.roll(group, 64, 1), group).astype(BF16)
    piece = (r // 16) * 4 + r % 4
    first_user = 8 * ((r % 16) // 4)

    @pl.loop(0, 8)
    def _(m):
        to = first_user + m

        @pl.when(to != r)
        def _():
            remote(gc_send, gc_recv.at[piece], gc_s.at[m], gc_r.at[piece], (f, to)).start()

        @pl.when(to == r)
        def _():
            gc_recv[piece] = gc_send[...]

    xs = conv(prior_i, raw[:, 0:256], [fi[k : k + 1] for k in range(4)], fib[...])
    step_raw = jnp.concatenate(
        [
            jnp.broadcast_to(raw[:, 576:577], (NSTEP * SLOTS, 128)),
            jnp.broadcast_to(raw[:, 577:578], (NSTEP * SLOTS, 128)),
        ],
        axis=1,
    )
    for load in loads[15:]:
        load.wait()

    def head_row(values):
        return jnp.where(lax.broadcasted_iota(jnp.int32, (1, 256), 1) < 128, values[0], values[1])

    v = step_raw + head_row(sb)
    dt = jnp.maximum(v, 0.0) + jnp.log1p(jnp.exp(-jnp.abs(v)))
    dec = jnp.exp(-dt * head_row(dr))
    dts = [dt[SLOTS * t : SLOTS * (t + 1)] for t in range(NSTEP)]
    decs = [dec[SLOTS * t : SLOTS * (t + 1)] for t in range(NSTEP)]

    @pl.loop(0, 8)
    def _(i):
        s = (i // 4) * 16 + 4 * (r // 8) + i % 4

        @pl.when(s != r)
        def _():
            remote(gc_send, gc_recv.at[i], gc_s.at[i], gc_r.at[i], (f, r)).wait_recv()

    def basis(i):
        return jnp.concatenate(
            [
                gc_recv[i].astype(F32) + gc_recv[i + 1].astype(F32),
                gc_recv[i + 2].astype(F32) + gc_recv[i + 3].astype(F32),
            ],
            axis=1,
        )

    b_all, c_all = basis(0), basis(4)
    bs = [b_all[SLOTS * t : SLOTS * (t + 1)] for t in range(NSTEP)]
    cs = [c_all[SLOTS * t : SLOTS * (t + 1)] for t in range(NSTEP)]
    us = [dts[t] * xs[t] for t in range(NSTEP)]
    ck[...] = jnp.zeros(ck.shape, F32)
    bk[...] = jnp.zeros(bk.shape, F32)
    uk[...] = jnp.zeros(uk.shape, F32)
    for t in range(NSTEP):
        ck[:, t, :] = cs[t]
        bk[:, t, :] = bs[t]
    tail = None
    for t in reversed(range(NSTEP)):
        uk[:, t, :] = us[t] if tail is None else us[t] * tail
        tail = decs[t] if tail is None else decs[t] * tail
    uk[:, 4, :] = tail

    gates = silu(raw[:, 256:512])
    fresh = []
    for t in range(NSTEP):
        total = None
        grown = None
        for s in reversed(range(t + 1)):
            pair = jnp.sum(bs[s] * cs[t], axis=1, keepdims=True)
            term = us[s] * pair
            if grown is not None:
                term = term * grown
            total = term if total is None else total + term
            grown = decs[s] if grown is None else grown * decs[s]
        fresh.append((total + head_row(sg) * xs[t], grown))

    @pl.loop(1, F)
    def _(o):
        s = source_of(f, o)
        for c in range(2):
            at = 2 * s + c
            remote(st_send.at[at], st_recv.at[at], st_s.at[at], st_r.at[at], (f, r)).wait_recv()

    @pl.loop(0, SLOTS)
    def _(q):
        j = jq[q]
        y = dot(ck[q].astype(BF16), st_recv[jnp.clip(j, 0, 2 * F - 1)], ((1,), (1,)))
        yk[q] = jnp.where(j >= 0, y, 0.0)

    gated = [
        (fresh[t][0] + fresh[t][1] * yk[:, t, :]) * gates[SLOTS * t : SLOTS * (t + 1)]
        for t in range(NSTEP)
    ]
    ga_all[f] = jnp.concatenate(gated, axis=0).astype(BF16)

    remote(ga_all.at[f], ga_all.at[f], ga_s.at[over], ga_r.at[f], (over, r)).start()

    def spread(block, sems):
        @pl.loop(0, Z - 1)
        def _(i):
            d = fy * Z + along(i)
            remote(ga_all.at[block], ga_all.at[block], sems.at[d], ga_r.at[block], (d, r)).start()

    def arrived(block):
        remote(ga_all.at[block], ga_all.at[block], ga_s.at[block], ga_r.at[block], (f, r)).wait_recv()

    spread(f, ga_s)
    arrived(over)
    spread(over, gf_s)

    @pl.loop(0, SLOTS)
    def _(q):
        j = jq[q]
        start = st_recv[jnp.clip(j, 0, 2 * F - 1)].astype(F32)
        start = jnp.where(j >= 0, start, 0.0)
        u = uk[q]
        rate = u[4:5]
        keep = lax.broadcasted_iota(jnp.int32, (8, 256), 0) < 4
        u = jnp.where(keep, u, 0.0)
        high = u.astype(BF16)
        low = (u - high.astype(F32)).astype(BF16)
        b = bk[q].astype(BF16)
        added = dot(
            jnp.concatenate([high, low], axis=0), jnp.concatenate([b, b], axis=0), ((0,), (0,))
        )
        for h in range(2):
            rows = slice(128 * h, 128 * h + 128)
            factor = jnp.concatenate([rate[:, rows], rate[:, rows]], axis=1)
            new_state[q, rows, :] = (start[rows] * factor + added[rows]).astype(BF16)


    def project_out(d):
        g = ga_all[d].astype(F32)
        squares = jnp.sum(g * g, axis=1, keepdims=True)
        part = dot((g * gain[...]).astype(BF16), wo[...], ((1,), (0,))).astype(BF16)
        where = lax.broadcasted_iota(jnp.int32, (16, 128), 1)
        high = squares.astype(BF16).astype(F32)
        low = squares - high
        for h in range(2):
            at = 32 * h
            lines = [
                jnp.where(where % 64 < 32, high[at + 16 * e : at + 16 * e + 16], low[at + 16 * e : at + 16 * e + 16])
                for e in range(2)
            ]
            squares_tile = jnp.where(where < 64, lines[0], lines[1]).astype(BF16)
            chunk = 2 * d + h
            po_send[chunk, 0:32, :] = part[at : at + 32, 0:128]
            po_send[chunk, 32:64, :] = part[at : at + 32, 128:256]
            po_send[chunk, 64:80, :] = squares_tile

            @pl.when(chunk != r)
            def _():
                remote(po_send.at[chunk], po_recv.at[r], po_s.at[chunk], po_r.at[r], (f, chunk)).start()

            @pl.when(chunk == r)
            def _():
                po_recv[r] = po_send[r]

    project_out(f)
    project_out(over)
    for y in range(2):

        @pl.loop(0, Z - 1)
        def _(i):
            block = jnp.where(y == 0, fy, 1 - fy) * Z + along(i)
            arrived(block)
            project_out(block)


    acc[0, 0:32, 0:256] = jnp.zeros((32, 256), F32)

    @pl.loop(0, 4)
    def _(g):
        acc[0, 32:64, 0:256] = jnp.zeros((32, 256), F32)
        ssum[...] = jnp.zeros((16, 128), F32)

        @pl.loop(0, 8)
        def _(i):
            s = 8 * g + i

            @pl.when(s != r)
            def _():
                remote(po_send.at[s], po_recv.at[s], po_s.at[s], po_r.at[s], (f, r)).wait_recv()

            acc[0, 32:64, 0:128] += po_recv[s, 0:32, :].astype(F32)
            acc[0, 32:64, 128:256] += po_recv[s, 32:64, :].astype(F32)
            ssum[...] += po_recv[s, 64:80, :].astype(F32)

        squares = ssum[...]
        squares = jnp.concatenate(
            [squares[:, 0:1] + squares[:, 32:33], squares[:, 64:65] + squares[:, 96:97]], axis=0
        )
        scale = lax.rsqrt(squares / (HPG * 128) + EPS)
        acc[0, 0:32, 0:256] += acc[0, 32:64, 0:256] * scale

    for k in range(2):
        fin_send[k] = acc[0, 0:32, 128 * k : 128 * k + 128].astype(BF16)

        @pl.when(jnp.logical_not(is_self(k)))
        def _():
            remote(
                fin_send.at[k], fin_recv.at[half], fin_s.at[k], fin_r.at[half], (home, 2 * f + k)
            ).start()

        @pl.when(is_self(k))
        def _():
            fin_recv[k] = fin_send[k]


    for k in range(2):

        @pl.when(jnp.logical_not(is_self(k)))
        def _():
            remote(fin_send.at[k], fin_recv.at[k], fin_s.at[k], fin_r.at[k], (f, r)).wait_recv()

        out[32 * k : 32 * k + 32, :] = fin_recv[k]

    for k in range(2):

        @pl.when(jnp.logical_not(is_self(k)))
        def _():
            remote(hid.at[pl.ds(0, 32)], hid_all.at[r, k], h1_s.at[k], h1_r.at[k], (f, r)).wait_send()
            remote(fin_send.at[k], fin_recv.at[k], fin_s.at[k], fin_r.at[k], (f, r)).wait_send()

    @pl.loop(1, R)
    def _(o):
        to = (r + o) % R
        remote(hid_all.at[r], hid_all.at[r], h2_s.at[to], h2_r.at[r], (f, r)).wait_send()
        remote(po_send.at[to], po_recv.at[r], po_s.at[to], po_r.at[r], (f, r)).wait_send()

    @pl.loop(1, F)
    def _(o):
        d = peer_of(f, o)
        remote(w_send.at[d], w_recv.at[f], w_s.at[d], w_r.at[f], (f, r)).wait_send()
        for c in range(2):
            at = 2 * d + c
            remote(st_send.at[at], st_recv.at[at], st_s.at[at], st_r.at[at], (f, r)).wait_send()

    across.wait_send()
    remote(ga_all.at[f], ga_all.at[f], ga_s.at[over], ga_r.at[f], (f, r)).wait_send()

    @pl.loop(0, Z - 1)
    def _(i):
        z = along(i)
        d = fy * Z + z
        remote(p_send.at[z], p_recv.at[fz], p_s.at[z], p_r.at[fz], (f, r)).wait_send()
        remote(ga_all.at[f], ga_all.at[f], ga_s.at[d], ga_r.at[f], (f, r)).wait_send()
        remote(ga_all.at[over], ga_all.at[over], gf_s.at[d], ga_r.at[over], (f, r)).wait_send()
        for c in range(2):
            at = 2 * z + c
            remote(relay.at[at], relay.at[at], rl_s.at[at], rl_r.at[at], (f, r)).wait_send()

    @pl.loop(0, 8)
    def _(m):
        @pl.when(first_user + m != r)
        def _():
            remote(gc_send, gc_recv.at[piece], gc_s.at[m], gc_r.at[piece], (f, r)).wait_send()


def mixer(*operands):
    vmem = pl.BlockSpec(memory_space=pltpu.VMEM)
    dma = pltpu.SemaphoreType.DMA
    pairs = [2, R, F, 2 * F, F, 8, F, R, 2, F, 1, F]
    held = [(pltpu.SMEM if x.ndim == 1 else pltpu.VMEM)(x.shape, x.dtype) for x in operands[:-1]]
    return pl.pallas_call(
        kernel,
        out_shape=(
            jax.ShapeDtypeStruct((64, 128), BF16),
            jax.ShapeDtypeStruct((SLOTS, 256, 256), BF16),
            jax.ShapeDtypeStruct((3, SLOTS, 256), BF16),
            jax.ShapeDtypeStruct((3, SLOTS, 64), BF16),
        ),
        in_specs=[pl.BlockSpec(memory_space=pl.ANY)] * len(operands),
        out_specs=(vmem,) * 4,
        scratch_shapes=held
        + [
            pltpu.VMEM((128, 256), BF16),
            pltpu.VMEM((8, 128), F32),
            pltpu.VMEM((SLOTS, 8, 128), F32),
            pltpu.VMEM((F, 16, 128), BF16),
            pltpu.VMEM((3, SLOTS, 128), F32),
            pltpu.VMEM((R, 2, 32, 128), BF16),
            pltpu.VMEM((Z, 2, 64, 640), BF16),
            pltpu.VMEM((Z, 2, 64, 640), BF16),
            pltpu.VMEM((F, 16, 128), BF16),
            pltpu.VMEM((F, 16, 128), F32),
            pltpu.VMEM((SLOTS, 256, 256), BF16),
            pltpu.VMEM((2 * F, 256, 256), BF16),
            pltpu.VMEM((2 * F, 256, 256), BF16),
            pltpu.VMEM((64, 128), BF16),
            pltpu.VMEM((8, 64, 128), BF16),
            pltpu.VMEM((F, 64, 256), BF16),
            pltpu.VMEM((R, 80, 128), BF16),
            pltpu.VMEM((R, 80, 128), BF16),
            pltpu.VMEM((2, 32, 128), BF16),
            pltpu.VMEM((2, 32, 128), BF16),
            pltpu.VMEM((2, 64, 640), F32),
            pltpu.VMEM((SLOTS, 8, 256), F32),
            pltpu.VMEM((SLOTS, 8, 256), F32),
            pltpu.VMEM((SLOTS, 8, 256), F32),
            pltpu.VMEM((SLOTS, 8, 256), F32),
            pltpu.VMEM((16, 128), F32),
            pltpu.SMEM((SLOTS,), jnp.int32),
            pltpu.SMEM((2 * F,), jnp.int32),
            pltpu.VMEM((2 * Z, 256, 256), BF16),
            pltpu.VMEM((64, 640), BF16),
            pltpu.VMEM((64, 640), BF16),
        ]
        + [dma((n,)) for n in pairs for _ in range(2)]
        + [dma((len(operands),))],
        compiler_params=pltpu.CompilerParams(
            collective_id=0, has_side_effects=True, vmem_limit_bytes=60 * 2**20
        ),
        name="mixer",
    )(*operands)


def on_device(
    hidden,
    inner_weight,
    gate_weight,
    group_weight,
    step_weight,
    output_weight,
    filter_inner,
    filter_inner_bias,
    filter_group,
    filter_group_bias,
    step_bias,
    decay_rate,
    skip_gain,
    norm_gain,
    recurrent_state,
    filter_inner_state,
    filter_group_state,
    live_counts,
    target_device,
    target_slot,
):
    out, new_state, win_i, win_g = mixer(
        live_counts,
        target_device,
        target_slot,
        step_bias,
        decay_rate,
        skip_gain,
        hidden.reshape(64, 128),
        inner_weight,
        gate_weight,
        group_weight.T,
        step_weight.T,
        output_weight,
        filter_inner,
        filter_inner_bias.reshape(1, 256),
        filter_group,
        filter_group_bias.reshape(1, 64),
        norm_gain.reshape(1, 256),
        jnp.transpose(filter_inner_state, (1, 0, 2)),
        jnp.transpose(filter_group_state, (1, 0, 2)),
        recurrent_state.reshape(SLOTS, 256, 256),
    )
    return (
        out.reshape(NSTEP, SLOTS, 128),
        new_state.reshape(SLOTS, 2, 128, 256),
        jnp.transpose(win_i, (1, 0, 2)),
        jnp.transpose(win_g, (1, 0, 2)),
    )


def solution(mesh):
    return jax.shard_map(
        on_device,
        mesh=mesh,
        in_specs=(
            P(None, "fsdp", "roll"),
            P("fsdp", "roll"),
            P("fsdp", "roll"),
            P("fsdp", "roll"),
            P("fsdp", "roll"),
            P("roll", "fsdp"),
            P(None, "roll"),
            P("roll"),
            P(None, "roll"),
            P("roll"),
            P("roll"),
            P("roll"),
            P("roll"),
            P("roll"),
            P("fsdp", "roll", None, None),
            P("fsdp", None, "roll"),
            P("fsdp", None, "roll"),
            P("fsdp"),
            P("fsdp"),
            P("fsdp"),
        ),
        out_specs=(
            P(None, "fsdp", "roll"),
            P("fsdp", "roll", None, None),
            P("fsdp", None, "roll"),
            P("fsdp", None, "roll"),
        ),
        check_vma=False,
    )
```

```python
import jax
import jax.numpy as jnp
from jax import lax
from jax.experimental import pallas as pl
from jax.experimental.pallas import tpu as pltpu
from jax.sharding import PartitionSpec as P

MESH = pl.DeviceIdType.MESH
F = 16
R = 32
Z = 8
HPG = 16
NSTEP = 4
SLOTS = 16
EPS = 1e-05
ALONG = (1, 7, 2, 6, 3, 5, 4)
ACROSS = (4, 3, 5, 2, 6, 1, 7, 0)
CROSS_ROWS = (0, 16, 0)
ALONG_ROWS = (0, 14, 0)
PASS_ROWS = (0, 14, 0)
F32 = jnp.float32
BF16 = jnp.bfloat16


def peer_of(f, o):
    return ((f // Z + o // Z) % 2) * Z + (f % Z + o % Z) % Z


def source_of(f, o):
    return ((f // Z + o // Z) % 2) * Z + (f % Z + Z - o % Z) % Z


def order(i):
    g, m = i // 4 + 1, i % 4
    near = (m // 2) * Z + jnp.where(m % 2 == 0, g, Z - g)
    return jnp.where(i < 12, near, jnp.where(i == 12, Z, 4 + Z * (i - 13)))


def silu(v):
    return v / (1.0 + jnp.exp(-v))


def dot(a, b, dims):
    return lax.dot_general(a, b, (dims, ((), ())), preferred_element_type=F32)


def kernel(
    live_h, td_h, ts_h, sb_h, dr_h, sg_h, hid_h, wi_h, wg_h, wgr_h, wst_h, wo_h, fi_h, fib_h, fg_h, fgb_h, gain_h,
    wini_h, wing_h, state,
    out, new_state, win_i, win_g,
    live, td, ts, sb, dr, sg, hid, wi, wg, wgr, wst, wo, fi, fib, fg, fgb, gain, wini, wing,
    wgs, gpar, win32, w_send, wg32,
    hid_all, p_send, p_recv, w_recv, w32, st_v, st_send, st_recv, gc_send, gc_recv,
    ga_all, po_send, po_recv, fin_send, fin_recv, acc, ck, bk, uk, yk, ssum, jq, pick, relay, py_send, py_recv, ph_send, ph_recv,
    h1_s, h1_r, h2_s, h2_r, w_s, w_r, st_s, st_r, p_s, p_r, gc_s, gc_r, ga_s, ga_r, po_s, po_r, fin_s, fin_r, rl_s, rl_r, py_s, py_r, gf_s, gf_r, ph_s, ph_r, loc,
):
    f = lax.axis_index("fsdp")
    r = lax.axis_index("roll")
    half = r % 2
    home = r // 2

    def remote(src, dst, s, d, device):
        return pltpu.make_async_remote_copy(
            src_ref=src, dst_ref=dst, send_sem=s, recv_sem=d, device_id=device, device_id_type=MESH
        )

    pairs = [
        (hid_h, hid), (td_h, td), (ts_h, ts), (live_h, live), (state, st_v), (wini_h, wini), (wing_h, wing),
        (wi_h, wi), (wg_h, wg), (wgr_h, wgr), (wst_h, wst), (fi_h, fi), (fib_h, fib), (fg_h, fg), (fgb_h, fgb),
        (sb_h, sb), (dr_h, dr), (sg_h, sg), (wo_h, wo), (gain_h, gain),
    ]
    loads = [pltpu.make_async_copy(a, b, loc.at[i]) for i, (a, b) in enumerate(pairs)]
    for load in loads:
        load.start()

    barrier = pltpu.get_barrier_semaphore()

    @pl.loop(1, F)
    def _(o):
        pl.semaphore_signal(barrier, inc=1, device_id=(peer_of(f, o), r), device_id_type=MESH)

    @pl.loop(1, R)
    def _(o):
        pl.semaphore_signal(barrier, inc=1, device_id=(f, (r + o) % R), device_id_type=MESH)

    def is_self(k):
        return (home == f) & (half == k)

    @pl.when(home != f)
    def _():
        for k in range(2):
            pl.semaphore_signal(barrier, inc=1, device_id=(home, 2 * f + k), device_id_type=MESH)

    for load in loads[1:4] + loads[5:15]:
        load.wait()
    wgs[...] = jnp.zeros((128, 256), BF16)
    wgs[0:64, :] = wgr[...]
    wgs[64:66, :] = wst[...]
    gpar[...] = jnp.zeros((8, 128), F32)
    gpar[0:4, 0:64] = fg[...]
    gpar[4:5, 0:64] = fgb[...]
    for k in range(3):
        win32[:, 2 * k, :] = wini[k, :, 0:128].astype(F32)
        win32[:, 2 * k + 1, :] = wini[k, :, 128:256].astype(F32)
    wg32[...] = jnp.zeros((3, SLOTS, 128), F32)
    for k in range(3):
        wg32[k, :, 0:64] = wing[k].astype(F32)
    win32[:, 6, :] = wg32[0] + pltpu.roll(wg32[1], 64, 1)
    win32[:, 7, :] = wg32[2]

    def picks(d):
        count = jnp.int32(0)
        got = [jnp.int32(0), jnp.int32(0)]
        to = [jnp.int32(-1), jnp.int32(-1)]
        for i in range(SLOTS):
            hit = (i < live[0]) & (td[i] == d)
            for c in range(2):
                mine = hit & (count == c)
                got[c] = jnp.where(mine, i, got[c])
                to[c] = jnp.where(mine, ts[i], to[c])
            count = count + jnp.where(hit, 1, 0)
        return got, to

    row8 = lax.broadcasted_iota(jnp.int32, (8, 128), 0)
    lane8 = lax.broadcasted_iota(jnp.int32, (8, 128), 1)

    @pl.loop(0, F)
    def _(d):
        got, to = picks(d)
        for c in range(2):
            pick[2 * d + c] = got[c]
        w_send[d] = jnp.concatenate(
            [
                jnp.where((row8 == 7) & (lane8 >= 64), to[c].astype(F32), win32[got[c]])
                for c in range(2)
            ],
            axis=0,
        ).astype(BF16)

    loads[4].wait()

    @pl.loop(0, 2 * F)
    def _(j):
        st_send[j] = st_v[pick[j]]

    for c in range(2):
        st_recv[2 * f + c] = st_send[2 * f + c]

    fy, fz = f // Z, f % Z
    over = (1 - fy) * Z + fz

    def turn(b):
        return (fz + jnp.where(half == 0, b, (Z - b) % Z)) % Z

    def upto(rows, point):
        return range(sum(rows[:point]), sum(rows[: point + 1]))

    def send_rows(point):
        for k in upto(CROSS_ROWS, point):
            c = k % 2
            z = turn(ACROSS[k // 2])
            at = 2 * ((1 - fy) * Z + z) + c
            if ACROSS[k // 2]:
                remote(st_send.at[at], relay.at[2 * z + c], st_s.at[at], rl_r.at[2 * z + c], (over, r)).start()
            else:
                remote(st_send.at[at], st_recv.at[2 * f + c], st_s.at[at], st_r.at[2 * f + c], (over, r)).start()
        for k in upto(ALONG_ROWS, point):
            d = fy * Z + turn(ALONG[k // 2])
            at, to = 2 * d + k % 2, 2 * f + k % 2
            remote(st_send.at[at], st_recv.at[to], st_s.at[at], st_r.at[to], (d, r)).start()
        for k in upto(PASS_ROWS, point):
            z = turn(ACROSS[k // 2])
            at, to = 2 * z + k % 2, 2 * over + k % 2
            remote(relay.at[at], relay.at[at], rl_s.at[at], rl_r.at[at], (f, r)).wait_recv()
            remote(relay.at[at], st_recv.at[to], rl_s.at[at], st_r.at[to], (fy * Z + z, r)).start()

    loads[0].wait()
    pl.semaphore_wait(barrier, F - 1 + R - 1 + jnp.where(home != f, 2, 0))

    for k in range(2):

        @pl.when(jnp.logical_not(is_self(k)))
        def _():
            remote(
                hid.at[pl.ds(32 * k, 32)], hid_all.at[2 * f + k, half], h1_s.at[k], h1_r.at[half],
                (home, 2 * f + k),
            ).start()

        @pl.when(is_self(k))
        def _():
            hid_all[r, k] = hid[pl.ds(32 * k, 32), :]

    @pl.loop(0, F - 1)
    def _(i):
        d = peer_of(f, order(i))
        remote(w_send.at[d], w_recv.at[f], w_s.at[d], w_r.at[f], (d, r)).start()

    w_recv[f] = w_send[f]

    send_rows(0)

    for k in range(2):

        @pl.when(jnp.logical_not(is_self(k)))
        def _():
            remote(hid.at[pl.ds(0, 32)], hid_all.at[r, k], h1_s.at[k], h1_r.at[k], (f, r)).wait_recv()

    @pl.loop(1, R)
    def _(o):
        to = (r + o) % R
        remote(hid_all.at[r], hid_all.at[r], h2_s.at[to], h2_r.at[r], (f, to)).start()

    send_rows(1)

    def project(z):
        chunks = [2 * (y * Z + z) + h for y in range(2) for h in range(2)]
        for chunk in chunks:

            @pl.when(chunk != r)
            def _():
                remote(
                    hid_all.at[chunk], hid_all.at[chunk], h2_s.at[chunk], h2_r.at[chunk], (f, r)
                ).wait_recv()

        rows = jnp.concatenate(
            [jnp.concatenate([hid_all[chunk, 0], hid_all[chunk, 1]], axis=1) for chunk in chunks],
            axis=0,
        )
        nn = ((1,), (0,))
        return (
            dot(rows, wi[...], nn),
            dot(rows, wg[...], nn),
            dot(rows, wgs[...], ((1,), (1,))),
        )

    def along(i):
        return (fz + jnp.where(i % 2 == half, i // 2 + 1, Z - 1 - i // 2)) % Z

    @pl.loop(0, Z - 1)
    def _(i):
        z = along(i)
        parts = project(z)
        for y in range(2):
            rows = slice(64 * y, 64 * y + 64)
            p_send[z, y, :, 0:256] = parts[0][rows].astype(BF16)
            p_send[z, y, :, 256:512] = parts[1][rows].astype(BF16)
            p_send[z, y, :, 512:640] = parts[2][rows].astype(BF16)
        remote(p_send.at[z], p_recv.at[fz], p_s.at[z], p_r.at[fz], (fy * Z + z, r)).start()

    send_rows(2)
    parts = project(fz)
    for y in range(2):
        rows = slice(64 * y, 64 * y + 64)
        acc[y, :, 0:256] = parts[0][rows]
        acc[y, :, 256:512] = parts[1][rows]
        acc[y, :, 512:640] = parts[2][rows]

    @pl.loop(1, F)
    def _(o):
        s = source_of(f, o)
        remote(w_send.at[s], w_recv.at[s], w_s.at[s], w_r.at[s], (f, r)).wait_recv()

    w32[...] = w_recv[...].astype(F32)
    lane = lax.broadcasted_iota(jnp.int32, (F, 128), 1)
    row = lax.broadcasted_iota(jnp.int32, (F, 128), 0)
    placers = []
    code = jnp.zeros((F, 128), F32)
    for c in range(2):
        slot = w32[:, 8 * c + 7, :][:, 64:65].astype(jnp.int32)
        hit = slot == lane
        placers.append(hit.astype(F32).astype(BF16))
        code = code + jnp.where(hit, (2 * row + c + 1).astype(F32), 0.0)

    @pl.loop(0, SLOTS)
    def _(q):
        jq[q] = jnp.sum(jnp.where(lane == q, code, 0.0)).astype(jnp.int32) - 1

    moved = []
    for block in range(8):
        total = jnp.zeros((128, 128), F32)
        for c in range(2):
            total = total + dot(placers[c], w32[:, 8 * c + block, :].astype(BF16), ((0,), (0,)))
        moved.append(total[0:SLOTS])
    prior_i = [jnp.concatenate([moved[2 * k], moved[2 * k + 1]], axis=1) for k in range(3)]
    prior_g = [moved[6], pltpu.roll(moved[6], 64, 1), moved[7]]

    @pl.loop(0, Z - 1)
    def _(i):
        z = along(i)
        remote(p_send.at[z], p_recv.at[z], p_s.at[z], p_r.at[z], (f, r)).wait_recv()
        acc[1 - fy] += p_recv[z, 1 - fy].astype(F32)

    py_send[...] = acc[1 - fy].astype(BF16)
    across = remote(py_send, py_recv, py_s.at[0], py_r.at[0], (over, r))
    across.start()

    @pl.loop(0, Z - 1)
    def _(i):
        acc[fy] += p_recv[along(i), fy].astype(F32)

    across.wait_recv()
    raw = (acc[fy] + py_recv[...].astype(F32)).astype(BF16)
    raw = raw.astype(F32)
    for t in range(1, NSTEP):
        rows = slice(SLOTS * t, SLOTS * (t + 1))
        win_i[t - 1] = raw[rows, 0:256].astype(BF16)
        win_g[t - 1] = raw[rows, 512:576].astype(BF16)

    def conv(prior, fresh, taps, bias):
        steps = prior + [fresh[SLOTS * t : SLOTS * (t + 1)] for t in range(NSTEP)]
        got = []
        for t in range(NSTEP):
            total = bias
            for k in range(4):
                total = total + taps[k] * steps[t + k]
            got.append(silu(total))
        return got

    group = jnp.concatenate(
        conv(prior_g, raw[:, 512:640], [gpar[k : k + 1] for k in range(4)], gpar[4:5]),
        axis=0,
    )
    gc_send[...] = jnp.where(half == 1, pltpu.roll(group, 64, 1), group).astype(BF16)
    piece = (r // 16) * 4 + r % 4
    first_user = 8 * ((r % 16) // 4)

    @pl.loop(0, 8)
    def _(m):
        to = first_user + m

        @pl.when(to != r)
        def _():
            remote(gc_send, gc_recv.at[piece], gc_s.at[m], gc_r.at[piece], (f, to)).start()

        @pl.when(to == r)
        def _():
            gc_recv[piece] = gc_send[...]

    xs = conv(prior_i, raw[:, 0:256], [fi[k : k + 1] for k in range(4)], fib[...])
    step_raw = jnp.concatenate(
        [
            jnp.broadcast_to(raw[:, 576:577], (NSTEP * SLOTS, 128)),
            jnp.broadcast_to(raw[:, 577:578], (NSTEP * SLOTS, 128)),
        ],
        axis=1,
    )
    for load in loads[15:]:
        load.wait()

    def head_row(values):
        return jnp.where(lax.broadcasted_iota(jnp.int32, (1, 256), 1) < 128, values[0], values[1])

    v = step_raw + head_row(sb)
    dt = jnp.maximum(v, 0.0) + jnp.log1p(jnp.exp(-jnp.abs(v)))
    dec = jnp.exp(-dt * head_row(dr))
    dts = [dt[SLOTS * t : SLOTS * (t + 1)] for t in range(NSTEP)]
    decs = [dec[SLOTS * t : SLOTS * (t + 1)] for t in range(NSTEP)]

    @pl.loop(0, 8)
    def _(i):
        s = (i // 4) * 16 + 4 * (r // 8) + i % 4

        @pl.when(s != r)
        def _():
            remote(gc_send, gc_recv.at[i], gc_s.at[i], gc_r.at[i], (f, r)).wait_recv()

    def basis(i):
        return jnp.concatenate(
            [
                gc_recv[i].astype(F32) + gc_recv[i + 1].astype(F32),
                gc_recv[i + 2].astype(F32) + gc_recv[i + 3].astype(F32),
            ],
            axis=1,
        )

    b_all, c_all = basis(0), basis(4)
    bs = [b_all[SLOTS * t : SLOTS * (t + 1)] for t in range(NSTEP)]
    cs = [c_all[SLOTS * t : SLOTS * (t + 1)] for t in range(NSTEP)]
    us = [dts[t] * xs[t] for t in range(NSTEP)]
    ck[...] = jnp.zeros(ck.shape, F32)
    bk[...] = jnp.zeros(bk.shape, F32)
    uk[...] = jnp.zeros(uk.shape, F32)
    for t in range(NSTEP):
        ck[:, t, :] = cs[t]
        bk[:, t, :] = bs[t]
    tail = None
    for t in reversed(range(NSTEP)):
        uk[:, t, :] = us[t] if tail is None else us[t] * tail
        tail = decs[t] if tail is None else decs[t] * tail
    uk[:, 4, :] = tail

    gates = silu(raw[:, 256:512])
    fresh = []
    for t in range(NSTEP):
        total = None
        grown = None
        for s in reversed(range(t + 1)):
            pair = jnp.sum(bs[s] * cs[t], axis=1, keepdims=True)
            term = us[s] * pair
            if grown is not None:
                term = term * grown
            total = term if total is None else total + term
            grown = decs[s] if grown is None else grown * decs[s]
        fresh.append((total + head_row(sg) * xs[t], grown))

    @pl.loop(1, F)
    def _(o):
        s = source_of(f, o)
        for c in range(2):
            at = 2 * s + c
            remote(st_send.at[at], st_recv.at[at], st_s.at[at], st_r.at[at], (f, r)).wait_recv()

    @pl.loop(0, SLOTS)
    def _(q):
        j = jq[q]
        y = dot(ck[q].astype(BF16), st_recv[jnp.clip(j, 0, 2 * F - 1)], ((1,), (1,)))
        yk[q] = jnp.where(j >= 0, y, 0.0)

    gated = [
        (fresh[t][0] + fresh[t][1] * yk[:, t, :]) * gates[SLOTS * t : SLOTS * (t + 1)]
        for t in range(NSTEP)
    ]
    ga_all[f] = jnp.concatenate(gated, axis=0).astype(BF16)

    remote(ga_all.at[f], ga_all.at[f], ga_s.at[over], ga_r.at[f], (over, r)).start()

    def spread(block, sems):
        @pl.loop(0, Z - 1)
        def _(i):
            d = fy * Z + along(i)
            remote(ga_all.at[block], ga_all.at[block], sems.at[d], ga_r.at[block], (d, r)).start()

    def arrived(block):
        remote(ga_all.at[block], ga_all.at[block], ga_s.at[block], ga_r.at[block], (f, r)).wait_recv()

    spread(f, ga_s)
    arrived(over)
    spread(over, gf_s)

    @pl.loop(0, SLOTS)
    def _(q):
        j = jq[q]
        start = st_recv[jnp.clip(j, 0, 2 * F - 1)].astype(F32)
        start = jnp.where(j >= 0, start, 0.0)
        u = uk[q]
        rate = u[4:5]
        keep = lax.broadcasted_iota(jnp.int32, (8, 256), 0) < 4
        u = jnp.where(keep, u, 0.0)
        high = u.astype(BF16)
        low = (u - high.astype(F32)).astype(BF16)
        b = bk[q].astype(BF16)
        added = dot(
            jnp.concatenate([high, low], axis=0), jnp.concatenate([b, b], axis=0), ((0,), (0,))
        )
        for h in range(2):
            rows = slice(128 * h, 128 * h + 128)
            factor = jnp.concatenate([rate[:, rows], rate[:, rows]], axis=1)
            new_state[q, rows, :] = (start[rows] * factor + added[rows]).astype(BF16)


    group_index, member = r // 8, r % 8

    def project_out(d):
        g = ga_all[d].astype(F32)
        squares = jnp.sum(g * g, axis=1, keepdims=True)
        part = dot((g * gain[...]).astype(BF16), wo[...], ((1,), (0,))).astype(BF16)
        where = lax.broadcasted_iota(jnp.int32, (16, 128), 1)
        high = squares.astype(BF16).astype(F32)
        low = squares - high
        for h in range(2):
            at = 32 * h
            lines = [
                jnp.where(where % 64 < 32, high[at + 16 * e : at + 16 * e + 16], low[at + 16 * e : at + 16 * e + 16])
                for e in range(2)
            ]
            squares_tile = jnp.where(where < 64, lines[0], lines[1]).astype(BF16)
            chunk = 2 * d + h
            po_send[chunk, 0:32, :] = part[at : at + 32, 0:128]
            po_send[chunk, 32:64, :] = part[at : at + 32, 128:256]
            po_send[chunk, 64:80, :] = squares_tile

            to = 8 * group_index + chunk % 8

            @pl.when(to != r)
            def _():
                slot = 4 * member + chunk // 8
                remote(po_send.at[chunk], po_recv.at[slot], po_s.at[chunk], po_r.at[slot], (f, to)).start()

            @pl.when(to == r)
            def _():
                po_recv[4 * member + chunk // 8] = po_send[chunk]

    project_out(f)
    project_out(over)
    for y in range(2):

        @pl.loop(0, Z - 1)
        def _(i):
            block = jnp.where(y == 0, fy, 1 - fy) * Z + along(i)
            arrived(block)
            project_out(block)


    @pl.loop(0, 4)
    def _(g):
        acc[0, 32:64, 0:256] = jnp.zeros((32, 256), F32)
        ssum[...] = jnp.zeros((16, 128), F32)

        @pl.loop(0, 8)
        def _(i):
            slot = 4 * i + g

            @pl.when(i != member)
            def _():
                remote(po_send.at[slot], po_recv.at[slot], po_s.at[slot], po_r.at[slot], (f, r)).wait_recv()

            acc[0, 32:64, 0:128] += po_recv[slot, 0:32, :].astype(F32)
            acc[0, 32:64, 128:256] += po_recv[slot, 32:64, :].astype(F32)
            ssum[...] += po_recv[slot, 64:80, :].astype(F32)

        squares = ssum[...]
        squares = jnp.concatenate(
            [squares[:, 0:1] + squares[:, 32:33], squares[:, 64:65] + squares[:, 96:97]], axis=0
        )
        scale = lax.rsqrt(squares / (HPG * 128) + EPS)
        scaled = (acc[0, 32:64, 0:256] * scale).astype(BF16)
        ph_send[g, 0:32, :] = scaled[:, 0:128]
        ph_send[g, 32:64, :] = scaled[:, 128:256]

        @pl.when(g != group_index)
        def _():
            remote(
                ph_send.at[g], ph_recv.at[group_index], ph_s.at[g], ph_r.at[group_index], (f, 8 * g + member)
            ).start()

        @pl.when(g == group_index)
        def _():
            ph_recv[g] = ph_send[g]

    acc[0, 0:32, 0:256] = jnp.zeros((32, 256), F32)

    @pl.loop(0, 4)
    def _(g):
        @pl.when(g != group_index)
        def _():
            remote(ph_send.at[g], ph_recv.at[g], ph_s.at[g], ph_r.at[g], (f, r)).wait_recv()

        acc[0, 0:32, 0:128] += ph_recv[g, 0:32, :].astype(F32)
        acc[0, 0:32, 128:256] += ph_recv[g, 32:64, :].astype(F32)

    for k in range(2):
        fin_send[k] = acc[0, 0:32, 128 * k : 128 * k + 128].astype(BF16)

        @pl.when(jnp.logical_not(is_self(k)))
        def _():
            remote(
                fin_send.at[k], fin_recv.at[half], fin_s.at[k], fin_r.at[half], (home, 2 * f + k)
            ).start()

        @pl.when(is_self(k))
        def _():
            fin_recv[k] = fin_send[k]


    for k in range(2):

        @pl.when(jnp.logical_not(is_self(k)))
        def _():
            remote(fin_send.at[k], fin_recv.at[k], fin_s.at[k], fin_r.at[k], (f, r)).wait_recv()

        out[32 * k : 32 * k + 32, :] = fin_recv[k]

    for k in range(2):

        @pl.when(jnp.logical_not(is_self(k)))
        def _():
            remote(hid.at[pl.ds(0, 32)], hid_all.at[r, k], h1_s.at[k], h1_r.at[k], (f, r)).wait_send()
            remote(fin_send.at[k], fin_recv.at[k], fin_s.at[k], fin_r.at[k], (f, r)).wait_send()

    @pl.loop(1, R)
    def _(o):
        to = (r + o) % R
        remote(hid_all.at[r], hid_all.at[r], h2_s.at[to], h2_r.at[r], (f, r)).wait_send()

    @pl.loop(1, F)
    def _(o):
        d = peer_of(f, o)
        remote(w_send.at[d], w_recv.at[f], w_s.at[d], w_r.at[f], (f, r)).wait_send()
        for c in range(2):
            at = 2 * d + c
            remote(st_send.at[at], st_recv.at[at], st_s.at[at], st_r.at[at], (f, r)).wait_send()

    @pl.loop(0, R)
    def _(chunk):
        @pl.when(chunk % 8 != member)
        def _():
            remote(po_send.at[chunk], po_recv.at[chunk], po_s.at[chunk], po_r.at[chunk], (f, r)).wait_send()

    @pl.loop(0, 4)
    def _(g):
        @pl.when(g != group_index)
        def _():
            remote(ph_send.at[g], ph_recv.at[g], ph_s.at[g], ph_r.at[g], (f, r)).wait_send()

    across.wait_send()
    remote(ga_all.at[f], ga_all.at[f], ga_s.at[over], ga_r.at[f], (f, r)).wait_send()

    @pl.loop(0, Z - 1)
    def _(i):
        z = along(i)
        d = fy * Z + z
        remote(p_send.at[z], p_recv.at[fz], p_s.at[z], p_r.at[fz], (f, r)).wait_send()
        remote(ga_all.at[f], ga_all.at[f], ga_s.at[d], ga_r.at[f], (f, r)).wait_send()
        remote(ga_all.at[over], ga_all.at[over], gf_s.at[d], ga_r.at[over], (f, r)).wait_send()
        for c in range(2):
            at = 2 * z + c
            remote(relay.at[at], relay.at[at], rl_s.at[at], rl_r.at[at], (f, r)).wait_send()

    @pl.loop(0, 8)
    def _(m):
        @pl.when(first_user + m != r)
        def _():
            remote(gc_send, gc_recv.at[piece], gc_s.at[m], gc_r.at[piece], (f, r)).wait_send()


def mixer(*operands):
    vmem = pl.BlockSpec(memory_space=pltpu.VMEM)
    dma = pltpu.SemaphoreType.DMA
    pairs = [2, R, F, 2 * F, F, 8, F, R, 2, F, 1, F, 4]
    held = [(pltpu.SMEM if x.ndim == 1 else pltpu.VMEM)(x.shape, x.dtype) for x in operands[:-1]]
    return pl.pallas_call(
        kernel,
        out_shape=(
            jax.ShapeDtypeStruct((64, 128), BF16),
            jax.ShapeDtypeStruct((SLOTS, 256, 256), BF16),
            jax.ShapeDtypeStruct((3, SLOTS, 256), BF16),
            jax.ShapeDtypeStruct((3, SLOTS, 64), BF16),
        ),
        in_specs=[pl.BlockSpec(memory_space=pl.ANY)] * len(operands),
        out_specs=(vmem,) * 4,
        scratch_shapes=held
        + [
            pltpu.VMEM((128, 256), BF16),
            pltpu.VMEM((8, 128), F32),
            pltpu.VMEM((SLOTS, 8, 128), F32),
            pltpu.VMEM((F, 16, 128), BF16),
            pltpu.VMEM((3, SLOTS, 128), F32),
            pltpu.VMEM((R, 2, 32, 128), BF16),
            pltpu.VMEM((Z, 2, 64, 640), BF16),
            pltpu.VMEM((Z, 2, 64, 640), BF16),
            pltpu.VMEM((F, 16, 128), BF16),
            pltpu.VMEM((F, 16, 128), F32),
            pltpu.VMEM((SLOTS, 256, 256), BF16),
            pltpu.VMEM((2 * F, 256, 256), BF16),
            pltpu.VMEM((2 * F, 256, 256), BF16),
            pltpu.VMEM((64, 128), BF16),
            pltpu.VMEM((8, 64, 128), BF16),
            pltpu.VMEM((F, 64, 256), BF16),
            pltpu.VMEM((R, 80, 128), BF16),
            pltpu.VMEM((R, 80, 128), BF16),
            pltpu.VMEM((2, 32, 128), BF16),
            pltpu.VMEM((2, 32, 128), BF16),
            pltpu.VMEM((2, 64, 640), F32),
            pltpu.VMEM((SLOTS, 8, 256), F32),
            pltpu.VMEM((SLOTS, 8, 256), F32),
            pltpu.VMEM((SLOTS, 8, 256), F32),
            pltpu.VMEM((SLOTS, 8, 256), F32),
            pltpu.VMEM((16, 128), F32),
            pltpu.SMEM((SLOTS,), jnp.int32),
            pltpu.SMEM((2 * F,), jnp.int32),
            pltpu.VMEM((2 * Z, 256, 256), BF16),
            pltpu.VMEM((64, 640), BF16),
            pltpu.VMEM((64, 640), BF16),
            pltpu.VMEM((4, 64, 128), BF16),
            pltpu.VMEM((4, 64, 128), BF16),
        ]
        + [dma((n,)) for n in pairs for _ in range(2)]
        + [dma((len(operands),))],
        compiler_params=pltpu.CompilerParams(
            collective_id=0, has_side_effects=True, vmem_limit_bytes=60 * 2**20
        ),
        name="mixer",
    )(*operands)


def on_device(
    hidden,
    inner_weight,
    gate_weight,
    group_weight,
    step_weight,
    output_weight,
    filter_inner,
    filter_inner_bias,
    filter_group,
    filter_group_bias,
    step_bias,
    decay_rate,
    skip_gain,
    norm_gain,
    recurrent_state,
    filter_inner_state,
    filter_group_state,
    live_counts,
    target_device,
    target_slot,
):
    out, new_state, win_i, win_g = mixer(
        live_counts,
        target_device,
        target_slot,
        step_bias,
        decay_rate,
        skip_gain,
        hidden.reshape(64, 128),
        inner_weight,
        gate_weight,
        group_weight.T,
        step_weight.T,
        output_weight,
        filter_inner,
        filter_inner_bias.reshape(1, 256),
        filter_group,
        filter_group_bias.reshape(1, 64),
        norm_gain.reshape(1, 256),
        jnp.transpose(filter_inner_state, (1, 0, 2)),
        jnp.transpose(filter_group_state, (1, 0, 2)),
        recurrent_state.reshape(SLOTS, 256, 256),
    )
    return (
        out.reshape(NSTEP, SLOTS, 128),
        new_state.reshape(SLOTS, 2, 128, 256),
        jnp.transpose(win_i, (1, 0, 2)),
        jnp.transpose(win_g, (1, 0, 2)),
    )


def solution(mesh):
    return jax.shard_map(
        on_device,
        mesh=mesh,
        in_specs=(
            P(None, "fsdp", "roll"),
            P("fsdp", "roll"),
            P("fsdp", "roll"),
            P("fsdp", "roll"),
            P("fsdp", "roll"),
            P("roll", "fsdp"),
            P(None, "roll"),
            P("roll"),
            P(None, "roll"),
            P("roll"),
            P("roll"),
            P("roll"),
            P("roll"),
            P("roll"),
            P("fsdp", "roll", None, None),
            P("fsdp", None, "roll"),
            P("fsdp", None, "roll"),
            P("fsdp"),
            P("fsdp"),
            P("fsdp"),
        ),
        out_specs=(
            P(None, "fsdp", "roll"),
            P("fsdp", "roll", None, None),
            P("fsdp", None, "roll"),
            P("fsdp", None, "roll"),
        ),
        check_vma=False,
    )
```

```python
import jax
import jax.numpy as jnp
from jax import lax
from jax.experimental import pallas as pl
from jax.experimental.pallas import tpu as pltpu
from jax.sharding import PartitionSpec as P

MESH = pl.DeviceIdType.MESH
F = 16
R = 32
Z = 8
HPG = 16
NSTEP = 4
SLOTS = 16
EPS = 1e-05
ALONG = (1, 7, 2, 6, 3, 5, 4)
ACROSS = (4, 3, 5, 2, 6, 1, 7, 0)
CROSS_ROWS = (4, 12, 0)
ALONG_ROWS = (8, 6, 0)
PASS_ROWS = (0, 14, 0)
F32 = jnp.float32
BF16 = jnp.bfloat16


def peer_of(f, o):
    return ((f // Z + o // Z) % 2) * Z + (f % Z + o % Z) % Z


def source_of(f, o):
    return ((f // Z + o // Z) % 2) * Z + (f % Z + Z - o % Z) % Z


def order(i):
    g, m = i // 4 + 1, i % 4
    near = (m // 2) * Z + jnp.where(m % 2 == 0, g, Z - g)
    return jnp.where(i < 12, near, jnp.where(i == 12, Z, 4 + Z * (i - 13)))


def silu(v):
    return v / (1.0 + jnp.exp(-v))


def dot(a, b, dims):
    return lax.dot_general(a, b, (dims, ((), ())), preferred_element_type=F32)


def kernel(
    live_h, td_h, ts_h, sb_h, dr_h, sg_h, hid_h, wi_h, wg_h, wgr_h, wst_h, wo_h, fi_h, fib_h, fg_h, fgb_h, gain_h,
    wini_h, wing_h, state,
    out, new_state, win_i, win_g,
    live, td, ts, sb, dr, sg, hid, wi, wg, wgr, wst, wo, fi, fib, fg, fgb, gain, wini, wing,
    wgs, gpar, win32, w_send, wg32,
    hid_all, p_send, p_recv, w_recv, w32, st_v, st_send, st_recv, gc_send, gc_recv,
    ga_all, po_send, po_recv, fin_send, fin_recv, acc, ck, bk, uk, yk, ssum, jq, pick, relay, py_send, py_recv, ph_send, ph_recv,
    h1_s, h1_r, h2_s, h2_r, w_s, w_r, st_s, st_r, p_s, p_r, gc_s, gc_r, ga_s, ga_r, po_s, po_r, fin_s, fin_r, rl_s, rl_r, py_s, py_r, gf_s, gf_r, ph_s, ph_r, loc,
):
    f = lax.axis_index("fsdp")
    r = lax.axis_index("roll")
    half = r % 2
    home = r // 2

    def remote(src, dst, s, d, device):
        return pltpu.make_async_remote_copy(
            src_ref=src, dst_ref=dst, send_sem=s, recv_sem=d, device_id=device, device_id_type=MESH
        )

    pairs = [
        (hid_h, hid), (td_h, td), (ts_h, ts), (live_h, live), (state, st_v), (wini_h, wini), (wing_h, wing),
        (wi_h, wi), (wg_h, wg), (wgr_h, wgr), (wst_h, wst), (fi_h, fi), (fib_h, fib), (fg_h, fg), (fgb_h, fgb),
        (sb_h, sb), (dr_h, dr), (sg_h, sg), (wo_h, wo), (gain_h, gain),
    ]
    loads = [pltpu.make_async_copy(a, b, loc.at[i]) for i, (a, b) in enumerate(pairs)]
    for load in loads:
        load.start()

    barrier = pltpu.get_barrier_semaphore()

    @pl.loop(1, F)
    def _(o):
        pl.semaphore_signal(barrier, inc=1, device_id=(peer_of(f, o), r), device_id_type=MESH)

    @pl.loop(1, R)
    def _(o):
        pl.semaphore_signal(barrier, inc=1, device_id=(f, (r + o) % R), device_id_type=MESH)

    def is_self(k):
        return (home == f) & (half == k)

    @pl.when(home != f)
    def _():
        for k in range(2):
            pl.semaphore_signal(barrier, inc=1, device_id=(home, 2 * f + k), device_id_type=MESH)

    for load in loads[1:4] + loads[5:15]:
        load.wait()
    wgs[...] = jnp.zeros((128, 256), BF16)
    wgs[0:64, :] = wgr[...]
    wgs[64:66, :] = wst[...]
    gpar[...] = jnp.zeros((8, 128), F32)
    gpar[0:4, 0:64] = fg[...]
    gpar[4:5, 0:64] = fgb[...]
    for k in range(3):
        win32[:, 2 * k, :] = wini[k, :, 0:128].astype(F32)
        win32[:, 2 * k + 1, :] = wini[k, :, 128:256].astype(F32)
    wg32[...] = jnp.zeros((3, SLOTS, 128), F32)
    for k in range(3):
        wg32[k, :, 0:64] = wing[k].astype(F32)
    win32[:, 6, :] = wg32[0] + pltpu.roll(wg32[1], 64, 1)
    win32[:, 7, :] = wg32[2]

    def picks(d):
        count = jnp.int32(0)
        got = [jnp.int32(0), jnp.int32(0)]
        to = [jnp.int32(-1), jnp.int32(-1)]
        for i in range(SLOTS):
            hit = (i < live[0]) & (td[i] == d)
            for c in range(2):
                mine = hit & (count == c)
                got[c] = jnp.where(mine, i, got[c])
                to[c] = jnp.where(mine, ts[i], to[c])
            count = count + jnp.where(hit, 1, 0)
        return got, to

    row8 = lax.broadcasted_iota(jnp.int32, (8, 128), 0)
    lane8 = lax.broadcasted_iota(jnp.int32, (8, 128), 1)

    @pl.loop(0, F)
    def _(d):
        got, to = picks(d)
        for c in range(2):
            pick[2 * d + c] = got[c]
        w_send[d] = jnp.concatenate(
            [
                jnp.where((row8 == 7) & (lane8 >= 64), to[c].astype(F32), win32[got[c]])
                for c in range(2)
            ],
            axis=0,
        ).astype(BF16)

    loads[4].wait()

    @pl.loop(0, 2 * F)
    def _(j):
        st_send[j] = st_v[pick[j]]

    for c in range(2):
        st_recv[2 * f + c] = st_send[2 * f + c]

    fy, fz = f // Z, f % Z
    over = (1 - fy) * Z + fz

    def turn(b):
        return (fz + jnp.where(half == 0, b, (Z - b) % Z)) % Z

    def upto(rows, point):
        return range(sum(rows[:point]), sum(rows[: point + 1]))

    def send_rows(point):
        for k in upto(CROSS_ROWS, point):
            c = k % 2
            z = turn(ACROSS[k // 2])
            at = 2 * ((1 - fy) * Z + z) + c
            if ACROSS[k // 2]:
                remote(st_send.at[at], relay.at[2 * z + c], st_s.at[at], rl_r.at[2 * z + c], (over, r)).start()
            else:
                remote(st_send.at[at], st_recv.at[2 * f + c], st_s.at[at], st_r.at[2 * f + c], (over, r)).start()
        for k in upto(ALONG_ROWS, point):
            d = fy * Z + turn(ALONG[k // 2])
            at, to = 2 * d + k % 2, 2 * f + k % 2
            remote(st_send.at[at], st_recv.at[to], st_s.at[at], st_r.at[to], (d, r)).start()
        for k in upto(PASS_ROWS, point):
            z = turn(ACROSS[k // 2])
            at, to = 2 * z + k % 2, 2 * over + k % 2
            remote(relay.at[at], relay.at[at], rl_s.at[at], rl_r.at[at], (f, r)).wait_recv()
            remote(relay.at[at], st_recv.at[to], rl_s.at[at], st_r.at[to], (fy * Z + z, r)).start()

    loads[0].wait()
    pl.semaphore_wait(barrier, F - 1 + R - 1 + jnp.where(home != f, 2, 0))

    for k in range(2):

        @pl.when(jnp.logical_not(is_self(k)))
        def _():
            remote(
                hid.at[pl.ds(32 * k, 32)], hid_all.at[2 * f + k, half], h1_s.at[k], h1_r.at[half],
                (home, 2 * f + k),
            ).start()

        @pl.when(is_self(k))
        def _():
            hid_all[r, k] = hid[pl.ds(32 * k, 32), :]

    @pl.loop(0, F - 1)
    def _(i):
        d = peer_of(f, order(i))
        remote(w_send.at[d], w_recv.at[f], w_s.at[d], w_r.at[f], (d, r)).start()

    w_recv[f] = w_send[f]

    send_rows(0)

    for k in range(2):

        @pl.when(jnp.logical_not(is_self(k)))
        def _():
            remote(hid.at[pl.ds(0, 32)], hid_all.at[r, k], h1_s.at[k], h1_r.at[k], (f, r)).wait_recv()

    @pl.loop(1, R)
    def _(o):
        to = (r + o) % R
        remote(hid_all.at[r], hid_all.at[r], h2_s.at[to], h2_r.at[r], (f, to)).start()

    send_rows(1)

    def project(z):
        chunks = [2 * (y * Z + z) + h for y in range(2) for h in range(2)]
        for chunk in chunks:

            @pl.when(chunk != r)
            def _():
                remote(
                    hid_all.at[chunk], hid_all.at[chunk], h2_s.at[chunk], h2_r.at[chunk], (f, r)
                ).wait_recv()

        rows = jnp.concatenate(
            [jnp.concatenate([hid_all[chunk, 0], hid_all[chunk, 1]], axis=1) for chunk in chunks],
            axis=0,
        )
        nn = ((1,), (0,))
        return (
            dot(rows, wi[...], nn),
            dot(rows, wg[...], nn),
            dot(rows, wgs[...], ((1,), (1,))),
        )

    def along(i):
        return (fz + jnp.where(i % 2 == half, i // 2 + 1, Z - 1 - i // 2)) % Z

    @pl.loop(0, Z - 1)
    def _(i):
        z = along(i)
        parts = project(z)
        for y in range(2):
            rows = slice(64 * y, 64 * y + 64)
            p_send[z, y, :, 0:256] = parts[0][rows].astype(BF16)
            p_send[z, y, :, 256:512] = parts[1][rows].astype(BF16)
            p_send[z, y, :, 512:640] = parts[2][rows].astype(BF16)
        remote(p_send.at[z], p_recv.at[fz], p_s.at[z], p_r.at[fz], (fy * Z + z, r)).start()

    send_rows(2)
    parts = project(fz)
    for y in range(2):
        rows = slice(64 * y, 64 * y + 64)
        acc[y, :, 0:256] = parts[0][rows]
        acc[y, :, 256:512] = parts[1][rows]
        acc[y, :, 512:640] = parts[2][rows]

    @pl.loop(1, F)
    def _(o):
        s = source_of(f, o)
        remote(w_send.at[s], w_recv.at[s], w_s.at[s], w_r.at[s], (f, r)).wait_recv()

    w32[...] = w_recv[...].astype(F32)
    lane = lax.broadcasted_iota(jnp.int32, (F, 128), 1)
    row = lax.broadcasted_iota(jnp.int32, (F, 128), 0)
    placers = []
    code = jnp.zeros((F, 128), F32)
    for c in range(2):
        slot = w32[:, 8 * c + 7, :][:, 64:65].astype(jnp.int32)
        hit = slot == lane
        placers.append(hit.astype(F32).astype(BF16))
        code = code + jnp.where(hit, (2 * row + c + 1).astype(F32), 0.0)

    @pl.loop(0, SLOTS)
    def _(q):
        jq[q] = jnp.sum(jnp.where(lane == q, code, 0.0)).astype(jnp.int32) - 1

    moved = []
    for block in range(8):
        total = jnp.zeros((128, 128), F32)
        for c in range(2):
            total = total + dot(placers[c], w32[:, 8 * c + block, :].astype(BF16), ((0,), (0,)))
        moved.append(total[0:SLOTS])
    prior_i = [jnp.concatenate([moved[2 * k], moved[2 * k + 1]], axis=1) for k in range(3)]
    prior_g = [moved[6], pltpu.roll(moved[6], 64, 1), moved[7]]

    @pl.loop(0, Z - 1)
    def _(i):
        z = along(i)
        remote(p_send.at[z], p_recv.at[z], p_s.at[z], p_r.at[z], (f, r)).wait_recv()
        acc[1 - fy] += p_recv[z, 1 - fy].astype(F32)

    py_send[...] = acc[1 - fy].astype(BF16)
    across = remote(py_send, py_recv, py_s.at[0], py_r.at[0], (over, r))
    across.start()

    @pl.loop(0, Z - 1)
    def _(i):
        acc[fy] += p_recv[along(i), fy].astype(F32)

    across.wait_recv()
    raw = (acc[fy] + py_recv[...].astype(F32)).astype(BF16)
    raw = raw.astype(F32)
    for t in range(1, NSTEP):
        rows = slice(SLOTS * t, SLOTS * (t + 1))
        win_i[t - 1] = raw[rows, 0:256].astype(BF16)
        win_g[t - 1] = raw[rows, 512:576].astype(BF16)

    def conv(prior, fresh, taps, bias):
        steps = prior + [fresh[SLOTS * t : SLOTS * (t + 1)] for t in range(NSTEP)]
        got = []
        for t in range(NSTEP):
            total = bias
            for k in range(4):
                total = total + taps[k] * steps[t + k]
            got.append(silu(total))
        return got

    group = jnp.concatenate(
        conv(prior_g, raw[:, 512:640], [gpar[k : k + 1] for k in range(4)], gpar[4:5]),
        axis=0,
    )
    gc_send[...] = jnp.where(half == 1, pltpu.roll(group, 64, 1), group).astype(BF16)
    piece = (r // 16) * 4 + r % 4
    first_user = 8 * ((r % 16) // 4)

    @pl.loop(0, 8)
    def _(m):
        to = first_user + m

        @pl.when(to != r)
        def _():
            remote(gc_send, gc_recv.at[piece], gc_s.at[m], gc_r.at[piece], (f, to)).start()

        @pl.when(to == r)
        def _():
            gc_recv[piece] = gc_send[...]

    xs = conv(prior_i, raw[:, 0:256], [fi[k : k + 1] for k in range(4)], fib[...])
    step_raw = jnp.concatenate(
        [
            jnp.broadcast_to(raw[:, 576:577], (NSTEP * SLOTS, 128)),
            jnp.broadcast_to(raw[:, 577:578], (NSTEP * SLOTS, 128)),
        ],
        axis=1,
    )
    for load in loads[15:]:
        load.wait()

    def head_row(values):
        return jnp.where(lax.broadcasted_iota(jnp.int32, (1, 256), 1) < 128, values[0], values[1])

    v = step_raw + head_row(sb)
    dt = jnp.maximum(v, 0.0) + jnp.log1p(jnp.exp(-jnp.abs(v)))
    dec = jnp.exp(-dt * head_row(dr))
    dts = [dt[SLOTS * t : SLOTS * (t + 1)] for t in range(NSTEP)]
    decs = [dec[SLOTS * t : SLOTS * (t + 1)] for t in range(NSTEP)]

    @pl.loop(0, 8)
    def _(i):
        s = (i // 4) * 16 + 4 * (r // 8) + i % 4

        @pl.when(s != r)
        def _():
            remote(gc_send, gc_recv.at[i], gc_s.at[i], gc_r.at[i], (f, r)).wait_recv()

    def basis(i):
        return jnp.concatenate(
            [
                gc_recv[i].astype(F32) + gc_recv[i + 1].astype(F32),
                gc_recv[i + 2].astype(F32) + gc_recv[i + 3].astype(F32),
            ],
            axis=1,
        )

    b_all, c_all = basis(0), basis(4)
    bs = [b_all[SLOTS * t : SLOTS * (t + 1)] for t in range(NSTEP)]
    cs = [c_all[SLOTS * t : SLOTS * (t + 1)] for t in range(NSTEP)]
    us = [dts[t] * xs[t] for t in range(NSTEP)]
    ck[...] = jnp.zeros(ck.shape, F32)
    bk[...] = jnp.zeros(bk.shape, F32)
    uk[...] = jnp.zeros(uk.shape, F32)
    for t in range(NSTEP):
        ck[:, t, :] = cs[t]
        bk[:, t, :] = bs[t]
    tail = None
    for t in reversed(range(NSTEP)):
        uk[:, t, :] = us[t] if tail is None else us[t] * tail
        tail = decs[t] if tail is None else decs[t] * tail
    uk[:, 4, :] = tail

    gates = silu(raw[:, 256:512])
    fresh = []
    for t in range(NSTEP):
        total = None
        grown = None
        for s in reversed(range(t + 1)):
            pair = jnp.sum(bs[s] * cs[t], axis=1, keepdims=True)
            term = us[s] * pair
            if grown is not None:
                term = term * grown
            total = term if total is None else total + term
            grown = decs[s] if grown is None else grown * decs[s]
        fresh.append((total + head_row(sg) * xs[t], grown))

    @pl.loop(1, F)
    def _(o):
        s = source_of(f, o)
        for c in range(2):
            at = 2 * s + c
            remote(st_send.at[at], st_recv.at[at], st_s.at[at], st_r.at[at], (f, r)).wait_recv()

    @pl.loop(0, SLOTS)
    def _(q):
        j = jq[q]
        y = dot(ck[q].astype(BF16), st_recv[jnp.clip(j, 0, 2 * F - 1)], ((1,), (1,)))
        yk[q] = jnp.where(j >= 0, y, 0.0)

    gated = [
        (fresh[t][0] + fresh[t][1] * yk[:, t, :]) * gates[SLOTS * t : SLOTS * (t + 1)]
        for t in range(NSTEP)
    ]
    ga_all[f] = jnp.concatenate(gated, axis=0).astype(BF16)

    remote(ga_all.at[f], ga_all.at[f], ga_s.at[over], ga_r.at[f], (over, r)).start()

    def spread(block, sems):
        @pl.loop(0, Z - 1)
        def _(i):
            d = fy * Z + along(i)
            remote(ga_all.at[block], ga_all.at[block], sems.at[d], ga_r.at[block], (d, r)).start()

    def arrived(block):
        remote(ga_all.at[block], ga_all.at[block], ga_s.at[block], ga_r.at[block], (f, r)).wait_recv()

    spread(f, ga_s)
    arrived(over)
    spread(over, gf_s)

    @pl.loop(0, SLOTS)
    def _(q):
        j = jq[q]
        start = st_recv[jnp.clip(j, 0, 2 * F - 1)].astype(F32)
        start = jnp.where(j >= 0, start, 0.0)
        u = uk[q]
        rate = u[4:5]
        keep = lax.broadcasted_iota(jnp.int32, (8, 256), 0) < 4
        u = jnp.where(keep, u, 0.0)
        high = u.astype(BF16)
        low = (u - high.astype(F32)).astype(BF16)
        b = bk[q].astype(BF16)
        added = dot(
            jnp.concatenate([high, low], axis=0), jnp.concatenate([b, b], axis=0), ((0,), (0,))
        )
        for h in range(2):
            rows = slice(128 * h, 128 * h + 128)
            factor = jnp.concatenate([rate[:, rows], rate[:, rows]], axis=1)
            new_state[q, rows, :] = (start[rows] * factor + added[rows]).astype(BF16)


    group_index, member = r // 8, r % 8

    def project_out(d):
        g = ga_all[d].astype(F32)
        squares = jnp.sum(g * g, axis=1, keepdims=True)
        part = dot((g * gain[...]).astype(BF16), wo[...], ((1,), (0,))).astype(BF16)
        where = lax.broadcasted_iota(jnp.int32, (16, 128), 1)
        high = squares.astype(BF16).astype(F32)
        low = squares - high
        for h in range(2):
            at = 32 * h
            lines = [
                jnp.where(where % 64 < 32, high[at + 16 * e : at + 16 * e + 16], low[at + 16 * e : at + 16 * e + 16])
                for e in range(2)
            ]
            squares_tile = jnp.where(where < 64, lines[0], lines[1]).astype(BF16)
            chunk = 2 * d + h
            po_send[chunk, 0:32, :] = part[at : at + 32, 0:128]
            po_send[chunk, 32:64, :] = part[at : at + 32, 128:256]
            po_send[chunk, 64:80, :] = squares_tile

            to = 8 * group_index + chunk % 8

            @pl.when(to != r)
            def _():
                slot = 4 * member + chunk // 8
                remote(po_send.at[chunk], po_recv.at[slot], po_s.at[chunk], po_r.at[slot], (f, to)).start()

            @pl.when(to == r)
            def _():
                po_recv[4 * member + chunk // 8] = po_send[chunk]

    project_out(f)
    project_out(over)
    for y in range(2):

        @pl.loop(0, Z - 1)
        def _(i):
            block = jnp.where(y == 0, fy, 1 - fy) * Z + along(i)
            arrived(block)
            project_out(block)


    @pl.loop(0, 4)
    def _(g):
        acc[0, 32:64, 0:256] = jnp.zeros((32, 256), F32)
        ssum[...] = jnp.zeros((16, 128), F32)

        @pl.loop(0, 8)
        def _(i):
            slot = 4 * i + g

            @pl.when(i != member)
            def _():
                remote(po_send.at[slot], po_recv.at[slot], po_s.at[slot], po_r.at[slot], (f, r)).wait_recv()

            acc[0, 32:64, 0:128] += po_recv[slot, 0:32, :].astype(F32)
            acc[0, 32:64, 128:256] += po_recv[slot, 32:64, :].astype(F32)
            ssum[...] += po_recv[slot, 64:80, :].astype(F32)

        squares = ssum[...]
        squares = jnp.concatenate(
            [squares[:, 0:1] + squares[:, 32:33], squares[:, 64:65] + squares[:, 96:97]], axis=0
        )
        scale = lax.rsqrt(squares / (HPG * 128) + EPS)
        scaled = (acc[0, 32:64, 0:256] * scale).astype(BF16)
        ph_send[g, 0:32, :] = scaled[:, 0:128]
        ph_send[g, 32:64, :] = scaled[:, 128:256]

        @pl.when(g != group_index)
        def _():
            remote(
                ph_send.at[g], ph_recv.at[group_index], ph_s.at[g], ph_r.at[group_index], (f, 8 * g + member)
            ).start()

        @pl.when(g == group_index)
        def _():
            ph_recv[g] = ph_send[g]

    acc[0, 0:32, 0:256] = jnp.zeros((32, 256), F32)

    @pl.loop(0, 4)
    def _(g):
        @pl.when(g != group_index)
        def _():
            remote(ph_send.at[g], ph_recv.at[g], ph_s.at[g], ph_r.at[g], (f, r)).wait_recv()

        acc[0, 0:32, 0:128] += ph_recv[g, 0:32, :].astype(F32)
        acc[0, 0:32, 128:256] += ph_recv[g, 32:64, :].astype(F32)

    for k in range(2):
        fin_send[k] = acc[0, 0:32, 128 * k : 128 * k + 128].astype(BF16)

        @pl.when(jnp.logical_not(is_self(k)))
        def _():
            remote(
                fin_send.at[k], fin_recv.at[half], fin_s.at[k], fin_r.at[half], (home, 2 * f + k)
            ).start()

        @pl.when(is_self(k))
        def _():
            fin_recv[k] = fin_send[k]


    @pl.loop(1, R)
    def _(o):
        to = (r + o) % R
        remote(hid_all.at[r], hid_all.at[r], h2_s.at[to], h2_r.at[r], (f, r)).wait_send()

    @pl.loop(1, F)
    def _(o):
        d = peer_of(f, o)
        remote(w_send.at[d], w_recv.at[f], w_s.at[d], w_r.at[f], (f, r)).wait_send()
        for c in range(2):
            at = 2 * d + c
            remote(st_send.at[at], st_recv.at[at], st_s.at[at], st_r.at[at], (f, r)).wait_send()

    @pl.loop(0, R)
    def _(chunk):
        @pl.when(chunk % 8 != member)
        def _():
            remote(po_send.at[chunk], po_recv.at[chunk], po_s.at[chunk], po_r.at[chunk], (f, r)).wait_send()

    @pl.loop(0, 4)
    def _(g):
        @pl.when(g != group_index)
        def _():
            remote(ph_send.at[g], ph_recv.at[g], ph_s.at[g], ph_r.at[g], (f, r)).wait_send()

    across.wait_send()
    remote(ga_all.at[f], ga_all.at[f], ga_s.at[over], ga_r.at[f], (f, r)).wait_send()

    @pl.loop(0, Z - 1)
    def _(i):
        z = along(i)
        d = fy * Z + z
        remote(p_send.at[z], p_recv.at[fz], p_s.at[z], p_r.at[fz], (f, r)).wait_send()
        remote(ga_all.at[f], ga_all.at[f], ga_s.at[d], ga_r.at[f], (f, r)).wait_send()
        remote(ga_all.at[over], ga_all.at[over], gf_s.at[d], ga_r.at[over], (f, r)).wait_send()
        for c in range(2):
            at = 2 * z + c
            remote(relay.at[at], relay.at[at], rl_s.at[at], rl_r.at[at], (f, r)).wait_send()

    @pl.loop(0, 8)
    def _(m):
        @pl.when(first_user + m != r)
        def _():
            remote(gc_send, gc_recv.at[piece], gc_s.at[m], gc_r.at[piece], (f, r)).wait_send()

    for k in range(2):

        @pl.when(jnp.logical_not(is_self(k)))
        def _():
            remote(fin_send.at[k], fin_recv.at[k], fin_s.at[k], fin_r.at[k], (f, r)).wait_recv()

        out[32 * k : 32 * k + 32, :] = fin_recv[k]

    for k in range(2):

        @pl.when(jnp.logical_not(is_self(k)))
        def _():
            remote(hid.at[pl.ds(0, 32)], hid_all.at[r, k], h1_s.at[k], h1_r.at[k], (f, r)).wait_send()
            remote(fin_send.at[k], fin_recv.at[k], fin_s.at[k], fin_r.at[k], (f, r)).wait_send()


def mixer(*operands):
    vmem = pl.BlockSpec(memory_space=pltpu.VMEM)
    dma = pltpu.SemaphoreType.DMA
    pairs = [2, R, F, 2 * F, F, 8, F, R, 2, F, 1, F, 4]
    held = [(pltpu.SMEM if x.ndim == 1 else pltpu.VMEM)(x.shape, x.dtype) for x in operands[:-1]]
    return pl.pallas_call(
        kernel,
        out_shape=(
            jax.ShapeDtypeStruct((64, 128), BF16),
            jax.ShapeDtypeStruct((SLOTS, 256, 256), BF16),
            jax.ShapeDtypeStruct((3, SLOTS, 256), BF16),
            jax.ShapeDtypeStruct((3, SLOTS, 64), BF16),
        ),
        in_specs=[pl.BlockSpec(memory_space=pl.ANY)] * len(operands),
        out_specs=(vmem,) * 4,
        scratch_shapes=held
        + [
            pltpu.VMEM((128, 256), BF16),
            pltpu.VMEM((8, 128), F32),
            pltpu.VMEM((SLOTS, 8, 128), F32),
            pltpu.VMEM((F, 16, 128), BF16),
            pltpu.VMEM((3, SLOTS, 128), F32),
            pltpu.VMEM((R, 2, 32, 128), BF16),
            pltpu.VMEM((Z, 2, 64, 640), BF16),
            pltpu.VMEM((Z, 2, 64, 640), BF16),
            pltpu.VMEM((F, 16, 128), BF16),
            pltpu.VMEM((F, 16, 128), F32),
            pltpu.VMEM((SLOTS, 256, 256), BF16),
            pltpu.VMEM((2 * F, 256, 256), BF16),
            pltpu.VMEM((2 * F, 256, 256), BF16),
            pltpu.VMEM((64, 128), BF16),
            pltpu.VMEM((8, 64, 128), BF16),
            pltpu.VMEM((F, 64, 256), BF16),
            pltpu.VMEM((R, 80, 128), BF16),
            pltpu.VMEM((R, 80, 128), BF16),
            pltpu.VMEM((2, 32, 128), BF16),
            pltpu.VMEM((2, 32, 128), BF16),
            pltpu.VMEM((2, 64, 640), F32),
            pltpu.VMEM((SLOTS, 8, 256), F32),
            pltpu.VMEM((SLOTS, 8, 256), F32),
            pltpu.VMEM((SLOTS, 8, 256), F32),
            pltpu.VMEM((SLOTS, 8, 256), F32),
            pltpu.VMEM((16, 128), F32),
            pltpu.SMEM((SLOTS,), jnp.int32),
            pltpu.SMEM((2 * F,), jnp.int32),
            pltpu.VMEM((2 * Z, 256, 256), BF16),
            pltpu.VMEM((64, 640), BF16),
            pltpu.VMEM((64, 640), BF16),
            pltpu.VMEM((4, 64, 128), BF16),
            pltpu.VMEM((4, 64, 128), BF16),
        ]
        + [dma((n,)) for n in pairs for _ in range(2)]
        + [dma((len(operands),))],
        compiler_params=pltpu.CompilerParams(
            collective_id=0, has_side_effects=True, vmem_limit_bytes=60 * 2**20
        ),
        name="mixer",
    )(*operands)


def on_device(
    hidden,
    inner_weight,
    gate_weight,
    group_weight,
    step_weight,
    output_weight,
    filter_inner,
    filter_inner_bias,
    filter_group,
    filter_group_bias,
    step_bias,
    decay_rate,
    skip_gain,
    norm_gain,
    recurrent_state,
    filter_inner_state,
    filter_group_state,
    live_counts,
    target_device,
    target_slot,
):
    out, new_state, win_i, win_g = mixer(
        live_counts,
        target_device,
        target_slot,
        step_bias,
        decay_rate,
        skip_gain,
        hidden.reshape(64, 128),
        inner_weight,
        gate_weight,
        group_weight.T,
        step_weight.T,
        output_weight,
        filter_inner,
        filter_inner_bias.reshape(1, 256),
        filter_group,
        filter_group_bias.reshape(1, 64),
        norm_gain.reshape(1, 256),
        jnp.transpose(filter_inner_state, (1, 0, 2)),
        jnp.transpose(filter_group_state, (1, 0, 2)),
        recurrent_state.reshape(SLOTS, 256, 256),
    )
    return (
        out.reshape(NSTEP, SLOTS, 128),
        new_state.reshape(SLOTS, 2, 128, 256),
        jnp.transpose(win_i, (1, 0, 2)),
        jnp.transpose(win_g, (1, 0, 2)),
    )


def solution(mesh):
    return jax.shard_map(
        on_device,
        mesh=mesh,
        in_specs=(
            P(None, "fsdp", "roll"),
            P("fsdp", "roll"),
            P("fsdp", "roll"),
            P("fsdp", "roll"),
            P("fsdp", "roll"),
            P("roll", "fsdp"),
            P(None, "roll"),
            P("roll"),
            P(None, "roll"),
            P("roll"),
            P("roll"),
            P("roll"),
            P("roll"),
            P("roll"),
            P("fsdp", "roll", None, None),
            P("fsdp", None, "roll"),
            P("fsdp", None, "roll"),
            P("fsdp"),
            P("fsdp"),
            P("fsdp"),
        ),
        out_specs=(
            P(None, "fsdp", "roll"),
            P("fsdp", "roll", None, None),
            P("fsdp", None, "roll"),
            P("fsdp", None, "roll"),
        ),
        check_vma=False,
    )
```
